1024 devices in a mesh: replica: 64 (over z_lo, y), tensor: 16 (over z_hi, x, core).
Axes of the slice: x: 4, y: 8, z: 16 (z_hi: 2, z_lo: 8; z = z_hi * 8 + z_lo), core: 2. Of those that a mesh axis runs over, the one named last changes fastest.
Arguments:
- hidden: bfloat16 [64, 256, 8192], P('replica', None, 'tensor'), may hold values from -6 to 6
- key_cotangent: bfloat16 [64, 256, 512], P('replica', 'tensor'), may hold values from -1.125 to 1.125
- key_weight: bfloat16 [64, 8192, 512], P('replica', 'tensor'), may hold values from -3 to 3
- first_moment: bfloat16 [64, 8192, 512], P('replica', 'tensor'), may hold values from -1.796875 to 1.796875
- second_moment: bfloat16 [64, 8192, 512], P('replica', 'tensor'), may hold values from 0.5 to 8
- local_fragment: bfloat16 [64, 1024, 512], P('replica', 'tensor'), may hold values from -6 to 6
- global_fragment: float32 [1024, 512], P('tensor'), may hold values from -6 to 6
- outer_momentum: float32 [1024, 512], P('tensor'), may hold values from -3 to 3
Outputs:
- new_weight: bfloat16 [64, 8192, 512], P('replica', 'tensor')
- new_first: bfloat16 [64, 8192, 512], P('replica', 'tensor')
- new_second: bfloat16 [64, 8192, 512], P('replica', 'tensor')
- new_global: float32 [1024, 512], P('tensor')
- new_momentum: float32 [1024, 512], P('tensor')
The draws below stay inside these ranges and needn't reach their ends.
All inputs are finite; a program needn't handle non-finite values.
Results may differ from the reference program's by a relative error of at most 0.001.
Values may be sent and summed in bfloat16 or wider, within the bound.
A program may use at most 32 MiB of HBM per device.

```python
import math
import jax
import jax.numpy as jnp
from jax import lax

D = 8192
KVW = 512
TOK = 256
ADAM_STEP = 4
REPLICAS = 64
FRAG_ROWS = 1024
N_REPLICA = 64


def shard_levels(rng, shape, split, least, top_value):
    loudness, own = 1.0, jax.random.fold_in(rng, 6)
    for position, shards_of in split:
        draws = jnp.exp(jax.random.uniform(jax.random.fold_in(own, position), (shards_of,), jnp.float32, least / len(split), top_value / len(split)))
        loudness = loudness * jnp.repeat(draws, shape[position] // shards_of).reshape([-1 if axis == position else 1 for axis in range(len(shape))])
    return loudness


def bell_draw(stream_key, extent, spread, most, cuts=(), kind=jnp.bfloat16):
    drawn = jax.random.normal(stream_key, extent, jnp.float32) * spread
    if len(cuts) > 0:
        drawn = shard_levels(stream_key, extent, cuts, -0.22, 0.18) * drawn
    return jnp.clip(drawn, min=-most, max=most).astype(kind)


def setup_inputs(seed: int = 0) -> dict:
    splits = jax.random.split(jax.random.key(seed), 9)
    return {
        "hidden": bell_draw(splits[0], (REPLICAS, TOK, D), 1.0, 6.0, ((0, 64), (2, 16))),
        "key_cotangent": bell_draw(splits[1], (REPLICAS, TOK, KVW), (3.0 / TOK ** 0.5), 1.125, ((0, 64), (1, 16))),
        "key_weight": bell_draw(splits[2], (REPLICAS, D, KVW), 0.5, 3.0, ((0, 64), (1, 16))),
        "first_moment": bell_draw(splits[3], (REPLICAS, D, KVW), 0.3, 1.796875, ((0, 64), (1, 16))),
        "second_moment": jnp.clip(jnp.exp(math.log(8.0) - 2.7725887 * jax.random.uniform(splits[4], (REPLICAS, D, KVW), jnp.float32) ** shard_levels(splits[4], (REPLICAS, D, KVW), ((0, 64), (1, 16)), -0.2, 0.2)), 0.5, 8.0).astype(jnp.bfloat16),
        "local_fragment": bell_draw(splits[5], (REPLICAS, FRAG_ROWS, KVW), 1.0, 6.0, ((0, 64), (1, 16))),
        "global_fragment": bell_draw(splits[6], (FRAG_ROWS, KVW), 1.0, 6.0, ((0, 16),), jnp.float32),
        "outer_momentum": bell_draw(splits[7], (FRAG_ROWS, KVW), 0.5, 3.0, ((0, 16),), jnp.float32),
    }


beta_one = 0.9
beta_two = 0.95
adam_eps = 1e-08
inner_rate = 0.01
decay_rate = 0.1
outer_rate = 0.7
outer_mu = 0.9

def inner_step(packed):
    acts, cotan, weight, first, second = packed
    grad = jnp.dot(acts.T, cotan, preferred_element_type=jnp.float32)
    first32 = beta_one * first.astype(jnp.float32) + (1.0 - beta_one) * grad
    second32 = beta_two * second.astype(jnp.float32) + (1.0 - beta_two) * grad * grad
    corr_one = 1.0 - beta_one ** ADAM_STEP
    corr_two = 1.0 - beta_two ** ADAM_STEP
    wfloat = weight.astype(jnp.float32)
    update = first32 / corr_one / (jnp.sqrt(second32 / corr_two) + adam_eps) + decay_rate * wfloat
    fresh = (wfloat - inner_rate * update).astype(jnp.bfloat16)
    return (fresh, first32.astype(jnp.bfloat16), second32.astype(jnp.bfloat16))

def reference(hidden, key_cotangent, key_weight, first_moment, second_moment, local_fragment, global_fragment, outer_momentum):
    new_weight, new_first, new_second = lax.map(inner_step, (hidden, key_cotangent, key_weight, first_moment, second_moment))
    total = lax.optimization_barrier(jnp.sum(global_fragment[None, :, :] - local_fragment.astype(jnp.float32), axis=0))
    delta = total / N_REPLICA
    new_momentum = outer_mu * outer_momentum + delta
    new_global = global_fragment - outer_rate * (delta + outer_mu * new_momentum)
    return (new_weight, new_first, new_second, new_global, new_momentum)
```

```python
import jax
import jax.numpy as jnp
from jax import lax
from jax.experimental import pallas as pl
from jax.experimental.pallas import tpu as pltpu
from jax.sharding import PartitionSpec as P

ADAM_STEP = 4
beta_one = 0.9
beta_two = 0.95
adam_eps = 1e-08
inner_rate = 0.01
decay_rate = 0.1
outer_rate = 0.7
outer_mu = 0.9
corr_one = 1.0 - beta_one**ADAM_STEP
corr_two = 1.0 - beta_two**ADAM_STEP

MESH = pl.DeviceIdType.MESH
NY, NZ, NX, NH, NC = 8, 8, 4, 2, 2
F32 = jnp.float32
BF16 = jnp.bfloat16


def kernel(
    h_hbm, k_hbm, w_hbm, m_hbm, v_hbm, l_hbm, g_hbm, o_hbm,
    nw_ref, nm_ref, nv_ref, ng_ref, no_ref,
    h, w, m, v, g, o, cot, yb, part, zb, zg, yg,
    load_sem, send_c, recv_c, send_f, recv_f,
):
    rep, ten = lax.axis_index("replica"), lax.axis_index("tensor")
    zl, y = rep // NY, lax.rem(rep, NY)
    zh, x, c = ten // (NX * NC), lax.rem(ten // NC, NX), lax.rem(ten, NC)

    def at_y(k):
        return (zl * NY + lax.rem(y + k, NY), ten)

    def at_z(k):
        return (lax.rem(zl + k, NZ) * NY + y, ten)

    def at_x(k):
        return (rep, zh * NX * NC + lax.rem(x + k, NX) * NC + c)

    at_h = (rep, (1 - zh) * NX * NC + x * NC + c)
    at_c = (rep, zh * NX * NC + x * NC + 1 - c)

    barrier = pltpu.get_barrier_semaphore()
    partners = [at_y(k) for k in range(1, NY)] + [at_z(k) for k in range(1, NZ)] + [at_x(k) for k in range(1, NX)] + [at_h, at_c]
    for partner in partners:
        pl.semaphore_signal(barrier, inc=1, device_id=partner, device_id_type=MESH)

    def chunk(k):
        yy = lax.rem(y + k, NY)
        return l_hbm.at[pl.ds(pl.multiple_of((yy // 2) * 16, 16), 16), pl.ds(pl.multiple_of(lax.rem(yy, 2) * 256, 256), 256)]

    loads = [
        pltpu.make_async_copy(src, dst, load_sem.at[i])
        for i, (src, dst) in enumerate(
            [
                (chunk(0), yb.at[y]),
                (k_hbm, cot.at[c, zh, x]),
                (h_hbm, h),
                (w_hbm, w),
                (m_hbm, m),
                (v_hbm, v),
                (g_hbm, g),
                (o_hbm, o),
            ]
        )
    ]
    for copy in loads:
        copy.start()
    pl.semaphore_wait(barrier, len(partners))

    started = []

    def send(src, dst, sems, i, device):
        copy = pltpu.make_async_remote_copy(
            src_ref=src, dst_ref=dst, send_sem=sems[0].at[i], recv_sem=sems[1].at[i], device_id=device, device_id_type=MESH
        )
        copy.start()
        started.append(copy)
        return copy

    sc, sf = (send_c, recv_c), (send_f, recv_f)
    mine = cot.at[c, zh, x]
    theirs = cot.at[c, 1 - zh, x]
    c_h = send(k_hbm, mine, sc, 0, at_h)
    f_y = [send(chunk(k), yb.at[y], sf, k - 1, at_y(k)) for k in range(1, NY)]
    c_x = [send(k_hbm, mine, sc, k, at_x(k)) for k in range(1, NX)]

    loads[0].wait()
    for copy in f_y:
        copy.wait_recv()
    total = yb[0].astype(F32)
    for i in range(1, NY):
        total += yb[i].astype(F32)
    for i in range(NZ):
        r, q, s = i // 4, (i // 2) % 2, i % 2
        part[i] = total[r * 8 + s * 4 : r * 8 + s * 4 + 4, q * 128 : q * 128 + 128]
    f_z = [send(part.at[lax.rem(zl + k, NZ)], zb.at[zl], sf, 7 + k - 1, at_z(k)) for k in range(1, NZ)]

    c_h.wait_recv()
    c_hx = [send(theirs, theirs, sc, 3 + k, at_x(k)) for k in range(1, NX)]

    loads[1].wait()
    for copy in c_x:
        copy.wait_recv()
    row = cot.at[c, zh]
    c_c = send(row, row, sc, 7, at_c)

    for copy in f_z:
        copy.wait_recv()
    zb[zl] = part[zl]
    total = zb[0]
    for i in range(1, NZ):
        total += zb[i]
    zg[zl] = total
    f_zg = [send(zg.at[zl], zg.at[zl], sf, 14 + k - 1, at_z(k)) for k in range(1, NZ)]

    for copy in c_hx:
        copy.wait_recv()
    row = cot.at[c, 1 - zh]
    c_hc = send(row, row, sc, 8, at_c)

    for copy in f_zg:
        copy.wait_recv()
    f_yg = [send(zg, yg.at[y], sf, 21 + k - 1, at_y(k)) for k in range(1, NY)]
    for i in range(NZ):
        yg[y, i] = zg[i]

    for copy in loads[2:6]:
        copy.wait()
    c_c.wait_recv()
    c_hc.wait_recv()
    keys = jnp.concatenate([cot[k, i, j] for i in range(NH) for j in range(NX) for k in range(NC)], axis=0)
    for i in range(4):
        rows = slice(i * 128, i * 128 + 128)
        grad = lax.dot_general(h[:, rows], keys, (((0,), (0,)), ((), ())), preferred_element_type=F32)
        first = beta_one * m[rows].astype(F32) + (1.0 - beta_one) * grad
        second = beta_two * v[rows].astype(F32) + (1.0 - beta_two) * grad * grad
        weight = w[rows].astype(F32)
        update = first / corr_one / (jnp.sqrt(second / corr_two) + adam_eps) + decay_rate * weight
        nw_ref[rows] = (weight - inner_rate * update).astype(BF16)
        nm_ref[rows] = first.astype(BF16)
        nv_ref[rows] = second.astype(BF16)

    for copy in loads[6:]:
        copy.wait()
    for copy in f_yg:
        copy.wait_recv()
    for j in range(NY):
        for i in range(NZ // 2):
            r = (j // 2) * 16 + (i // 2) * 8
            q = (j % 2) * 256 + (i % 2) * 128
            area = (slice(r, r + 8), slice(q, q + 128))
            total = jnp.concatenate([yg[j, 2 * i], yg[j, 2 * i + 1]], axis=0)
            delta = g[area] - total * (1.0 / (NY * NZ))
            fresh = outer_mu * o[area] + delta
            no_ref[area] = fresh
            ng_ref[area] = g[area] - outer_rate * (delta + outer_mu * fresh)

    for copy in started:
        copy.wait_send()


def store_kernel(*refs):
    sems = refs[10]
    copies = [pltpu.make_async_copy(refs[i], refs[5 + i], sems.at[i]) for i in range(5)]
    for copy in copies:
        copy.start()
    for copy in copies:
        copy.wait()


def per_device(hidden, cotangent, weight, first, second, local, glob, momentum):
    hidden, cotangent, weight, first, second, local = (a[0] for a in (hidden, cotangent, weight, first, second, local))
    args = (hidden, cotangent, weight, first, second, local, glob, momentum)
    (tok, d), (ktok, kv), (rows, _) = hidden.shape, cotangent.shape, glob.shape
    vm = pl.BlockSpec(memory_space=pltpu.VMEM)
    out = pl.pallas_call(
        kernel,
        out_shape=[
            jax.ShapeDtypeStruct((d, kv), BF16),
            jax.ShapeDtypeStruct((d, kv), BF16),
            jax.ShapeDtypeStruct((d, kv), BF16),
            jax.ShapeDtypeStruct((rows, kv), F32),
            jax.ShapeDtypeStruct((rows, kv), F32),
        ],
        in_specs=[pl.BlockSpec(memory_space=pltpu.HBM)] * 8,
        out_specs=[vm] * 5,
        scratch_shapes=[
            pltpu.VMEM((tok, d), BF16),
            pltpu.VMEM((d, kv), BF16),
            pltpu.VMEM((d, kv), BF16),
            pltpu.VMEM((d, kv), BF16),
            pltpu.VMEM((rows, kv), F32),
            pltpu.VMEM((rows, kv), F32),
            pltpu.VMEM((NC, NH, NX, ktok, kv), BF16),
            pltpu.VMEM((NY, 16, 256), BF16),
            pltpu.VMEM((NZ, 4, 128), F32),
            pltpu.VMEM((NZ, 4, 128), F32),
            pltpu.VMEM((NZ, 4, 128), F32),
            pltpu.VMEM((NY, NZ, 4, 128), F32),
            pltpu.SemaphoreType.DMA((8,)),
            pltpu.SemaphoreType.DMA((9,)),
            pltpu.SemaphoreType.DMA((9,)),
            pltpu.SemaphoreType.DMA((28,)),
            pltpu.SemaphoreType.DMA((28,)),
        ],
        compiler_params=pltpu.CompilerParams(
            collective_id=0, has_side_effects=True, vmem_limit_bytes=24 * 1024 * 1024
        ),
    )(*(pltpu.with_memory_space_constraint(a, pltpu.HBM) for a in args))
    out = pl.pallas_call(
        store_kernel,
        out_shape=[jax.ShapeDtypeStruct(a.shape, a.dtype) for a in out],
        in_specs=[vm] * 5,
        out_specs=[pl.BlockSpec(memory_space=pltpu.HBM)] * 5,
        scratch_shapes=[pltpu.SemaphoreType.DMA((5,))],
    )(*out)
    return (out[0][None], out[1][None], out[2][None], out[3], out[4])


def solution(mesh):
    return jax.shard_map(
        per_device,
        mesh=mesh,
        in_specs=(
            P("replica", None, "tensor"),
            P("replica", "tensor", None),
            P("replica", "tensor", None),
            P("replica", "tensor", None),
            P("replica", "tensor", None),
            P("replica", "tensor", None),
            P("tensor", None),
            P("tensor", None),
        ),
        out_specs=(
            P("replica", "tensor", None),
            P("replica", "tensor", None),
            P("replica", "tensor", None),
            P("tensor", None),
            P("tensor", None),
        ),
        check_vma=False,
    )
```

```python
import jax
import jax.numpy as jnp
from jax import lax
from jax.experimental import pallas as pl
from jax.experimental.pallas import tpu as pltpu
from jax.sharding import PartitionSpec as P

ADAM_STEP = 4
beta_one = 0.9
beta_two = 0.95
adam_eps = 1e-08
inner_rate = 0.01
decay_rate = 0.1
outer_rate = 0.7
outer_mu = 0.9
corr_one = 1.0 - beta_one**ADAM_STEP
corr_two = 1.0 - beta_two**ADAM_STEP

MESH = pl.DeviceIdType.MESH
NY, NZ, NX, NH, NC = 8, 8, 4, 2, 2
F32 = jnp.float32
BF16 = jnp.bfloat16


def kernel(
    h_hbm, k_hbm, w_hbm, m_hbm, v_hbm, l_hbm, g_hbm, o_hbm,
    nw_ref, nm_ref, nv_ref, ng_ref, no_ref,
    h, w, m, v, g, o, cot, raw, part, sums, whole,
    load_sem, send_c, recv_c, send_r, recv_r, send_s, recv_s, send_w, recv_w,
):
    rep, ten = lax.axis_index("replica"), lax.axis_index("tensor")
    zl, y = rep // NY, lax.rem(rep, NY)
    zh, x, c = ten // (NX * NC), lax.rem(ten // NC, NX), lax.rem(ten, NC)
    pair, side = zl // 2, lax.rem(zl, 2)
    me = y * 2 + side

    near = sorted(((k, e) for k in range(NY) for e in range(2) if k + e > 0), key=lambda t: -(min(t[0], NY - t[0]) + t[1]))

    def place(k, e):
        return lax.rem(y + k, NY), (1 - side if e else side)

    def at_near(k, e):
        yy, ss = place(k, e)
        return ((pair * 2 + ss) * NY + yy, ten)

    def at_pair(k):
        return ((lax.rem(pair + k, NZ // 2) * 2 + side) * NY + y, ten)

    def at_x(k):
        return (rep, zh * NX * NC + lax.rem(x + k, NX) * NC + c)

    at_h = (rep, (1 - zh) * NX * NC + x * NC + c)
    at_c = (rep, zh * NX * NC + x * NC + 1 - c)

    barrier = pltpu.get_barrier_semaphore()
    partners = [at_h] + [at_pair(k) for k in range(1, NZ // 2)] + [at_near(*t) for t in near] + [at_x(k) for k in (2, 1, 3)] + [at_c]
    for partner in partners:
        pl.semaphore_signal(barrier, inc=1, device_id=partner, device_id_type=MESH)

    def chunk(k, e):
        yy, ss = place(k, e)
        i = yy * 2 + ss
        return l_hbm.at[pl.ds(pl.multiple_of((i // 4) * 16, 16), 16), pl.ds(pl.multiple_of(lax.rem(i, 4) * 128, 128), 128)]

    loads = [
        pltpu.make_async_copy(src, dst, load_sem.at[i])
        for i, (src, dst) in enumerate(
            [
                (chunk(0, 0), raw.at[me]),
                (k_hbm, cot.at[c, zh, x]),
                (h_hbm, h),
                (w_hbm, w),
                (m_hbm, m),
                (v_hbm, v),
                (g_hbm, g),
                (o_hbm, o),
            ]
        )
    ]
    for copy in loads:
        copy.start()
    pl.semaphore_wait(barrier, len(partners))

    started = []

    def send(src, dst, sends, recvs, i, device):
        copy = pltpu.make_async_remote_copy(
            src_ref=src, dst_ref=dst, send_sem=sends.at[i], recv_sem=recvs.at[i], device_id=device, device_id_type=MESH
        )
        copy.start()
        started.append(copy)
        return copy

    mine = cot.at[c, zh, x]
    theirs = cot.at[c, 1 - zh, x]
    c_h = send(k_hbm, mine, send_c, recv_c, 0, at_h)
    f_raw = [send(chunk(*t), raw.at[me], send_r, recv_r, t[0] * 2 + t[1] - 1, at_near(*t)) for t in near]
    c_x = [send(k_hbm, mine, send_c, recv_c, k, at_x(k)) for k in (2, 1, 3)]

    loads[0].wait()
    for copy in f_raw:
        copy.wait_recv()
    total = raw[0].astype(F32)
    for i in range(1, 2 * NY):
        total += raw[i].astype(F32)
    part[...] = total
    f_sum = [send(part, sums.at[pair], send_s, recv_s, k - 1, at_pair(k)) for k in range(1, NZ // 2)]
    sums[pair] = total

    c_h.wait_recv()
    c_hx = [send(theirs, theirs, send_c, recv_c, 3 + k, at_x(k)) for k in (2, 1, 3)]

    loads[1].wait()
    for copy in c_x:
        copy.wait_recv()
    row = cot.at[c, zh]
    c_c = send(row, row, send_c, recv_c, 7, at_c)

    for copy in f_sum:
        copy.wait_recv()
    total = sums[0]
    for i in range(1, NZ // 2):
        total += sums[i]
    whole[me] = total
    f_whole = [send(whole.at[me], whole.at[me], send_w, recv_w, t[0] * 2 + t[1] - 1, at_near(*t)) for t in near]

    for copy in c_hx:
        copy.wait_recv()
    row = cot.at[c, 1 - zh]
    c_hc = send(row, row, send_c, recv_c, 8, at_c)

    for copy in loads[2:6]:
        copy.wait()
    c_c.wait_recv()
    c_hc.wait_recv()
    keys = jnp.concatenate([cot[k, i, j] for i in range(NH) for j in range(NX) for k in range(NC)], axis=0)
    for i in range(4):
        rows = slice(i * 128, i * 128 + 128)
        grad = lax.dot_general(h[:, rows], keys, (((0,), (0,)), ((), ())), preferred_element_type=F32)
        first = beta_one * m[rows].astype(F32) + (1.0 - beta_one) * grad
        second = beta_two * v[rows].astype(F32) + (1.0 - beta_two) * grad * grad
        weight = w[rows].astype(F32)
        update = first / corr_one / (jnp.sqrt(second / corr_two) + adam_eps) + decay_rate * weight
        nw_ref[rows] = (weight - inner_rate * update).astype(BF16)
        nm_ref[rows] = first.astype(BF16)
        nv_ref[rows] = second.astype(BF16)

    for copy in loads[6:]:
        copy.wait()
    for copy in f_whole:
        copy.wait_recv()
    for i in range(2 * NY):
        r, q = (i // 4) * 16, (i % 4) * 128
        area = (slice(r, r + 16), slice(q, q + 128))
        delta = g[area] - whole[i] * (1.0 / (NY * NZ))
        fresh = outer_mu * o[area] + delta
        no_ref[area] = fresh
        ng_ref[area] = g[area] - outer_rate * (delta + outer_mu * fresh)

    for copy in started:
        copy.wait_send()


def store_kernel(*refs):
    sems = refs[10]
    copies = [pltpu.make_async_copy(refs[i], refs[5 + i], sems.at[i]) for i in range(5)]
    for copy in copies:
        copy.start()
    for copy in copies:
        copy.wait()


def per_device(hidden, cotangent, weight, first, second, local, glob, momentum):
    hidden, cotangent, weight, first, second, local = (a[0] for a in (hidden, cotangent, weight, first, second, local))
    args = (hidden, cotangent, weight, first, second, local, glob, momentum)
    (tok, d), (ktok, kv), (rows, _) = hidden.shape, cotangent.shape, glob.shape
    vm = pl.BlockSpec(memory_space=pltpu.VMEM)
    out = pl.pallas_call(
        kernel,
        out_shape=[
            jax.ShapeDtypeStruct((d, kv), BF16),
            jax.ShapeDtypeStruct((d, kv), BF16),
            jax.ShapeDtypeStruct((d, kv), BF16),
            jax.ShapeDtypeStruct((rows, kv), F32),
            jax.ShapeDtypeStruct((rows, kv), F32),
        ],
        in_specs=[pl.BlockSpec(memory_space=pltpu.HBM)] * 8,
        out_specs=[vm] * 5,
        scratch_shapes=[
            pltpu.VMEM((tok, d), BF16),
            pltpu.VMEM((d, kv), BF16),
            pltpu.VMEM((d, kv), BF16),
            pltpu.VMEM((d, kv), BF16),
            pltpu.VMEM((rows, kv), F32),
            pltpu.VMEM((rows, kv), F32),
            pltpu.VMEM((NC, NH, NX, ktok, kv), BF16),
            pltpu.VMEM((2 * NY, 16, 128), BF16),
            pltpu.VMEM((16, 128), F32),
            pltpu.VMEM((NZ // 2, 16, 128), F32),
            pltpu.VMEM((2 * NY, 16, 128), F32),
            pltpu.SemaphoreType.DMA((8,)),
            pltpu.SemaphoreType.DMA((9,)),
            pltpu.SemaphoreType.DMA((9,)),
            pltpu.SemaphoreType.DMA((15,)),
            pltpu.SemaphoreType.DMA((15,)),
            pltpu.SemaphoreType.DMA((3,)),
            pltpu.SemaphoreType.DMA((3,)),
            pltpu.SemaphoreType.DMA((15,)),
            pltpu.SemaphoreType.DMA((15,)),
        ],
        compiler_params=pltpu.CompilerParams(
            collective_id=0, has_side_effects=True, vmem_limit_bytes=16 * 1024 * 1024
        ),
    )(*(pltpu.with_memory_space_constraint(a, pltpu.HBM) for a in args))
    out = pl.pallas_call(
        store_kernel,
        out_shape=[jax.ShapeDtypeStruct(a.shape, a.dtype) for a in out],
        in_specs=[vm] * 5,
        out_specs=[pl.BlockSpec(memory_space=pltpu.HBM)] * 5,
        scratch_shapes=[pltpu.SemaphoreType.DMA((5,))],
        compiler_params=pltpu.CompilerParams(vmem_limit_bytes=4 * 1024 * 1024),
    )(*out)
    return (out[0][None], out[1][None], out[2][None], out[3], out[4])


def solution(mesh):
    return jax.shard_map(
        per_device,
        mesh=mesh,
        in_specs=(
            P("replica", None, "tensor"),
            P("replica", "tensor", None),
            P("replica", "tensor", None),
            P("replica", "tensor", None),
            P("replica", "tensor", None),
            P("replica", "tensor", None),
            P("tensor", None),
            P("tensor", None),
        ),
        out_specs=(
            P("replica", "tensor", None),
            P("replica", "tensor", None),
            P("replica", "tensor", None),
            P("tensor", None),
            P("tensor", None),
        ),
        check_vma=False,
    )
```

```python
import jax
import jax.numpy as jnp
from jax import lax
from jax.experimental import pallas as pl
from jax.experimental.pallas import tpu as pltpu
from jax.sharding import PartitionSpec as P

ADAM_STEP = 4
beta_one = 0.9
beta_two = 0.95
adam_eps = 1e-08
inner_rate = 0.01
decay_rate = 0.1
outer_rate = 0.7
outer_mu = 0.9
corr_one = 1.0 - beta_one**ADAM_STEP
corr_two = 1.0 - beta_two**ADAM_STEP

MESH = pl.DeviceIdType.MESH
NY, NZ, NX, NH, NC = 8, 8, 4, 2, 2
NR = 2
F32 = jnp.float32
BF16 = jnp.bfloat16


def kernel(
    h_hbm, k_hbm, w_hbm, m_hbm, v_hbm, l_hbm, g_hbm, o_hbm,
    nw_ref, nm_ref, nv_ref, ng_ref, no_ref,
    h, w, m, v, g, o, cot, raw, whole,
    load_sem, send_c, recv_c, send_r, recv_r, send_w, recv_w, send_z, recv_z, send_y, recv_y, ready,
):
    rep, ten = lax.axis_index("replica"), lax.axis_index("tensor")
    zl, y = rep // NY, lax.rem(rep, NY)
    zh, x, c = ten // (NX * NC), lax.rem(ten // NC, NX), lax.rem(ten, NC)
    side = lax.rem(zl, NR)
    reducer = zl < NR
    me = y * NR + side

    near = sorted(((k, e) for k in range(NY) for e in range(NR) if k + e > 0), key=lambda t: -(min(t[0], NY - t[0]) + t[1]))

    def place(k, e):
        return lax.rem(y + k, NY), (1 - side if e else side)

    def at_near(k, e):
        yy, ss = place(k, e)
        return (ss * NY + yy, ten)

    def at_y(k):
        return (zl * NY + lax.rem(y + k, NY), ten)

    def at_x(k, other=False):
        return (rep, zh * NX * NC + lax.rem(x + k, NX) * NC + (1 - c if other else c))

    at_h = (rep, (1 - zh) * NX * NC + x * NC + c)

    barrier = pltpu.get_barrier_semaphore()

    @pl.when(zh == 0)
    def _():
        pl.semaphore_signal(barrier, inc=1, device_id=at_h, device_id_type=MESH)

    peers = [at_x(k, other) for k in (2, 1, 3, 0) for other in (False, True) if k or other]
    for peer in peers:
        pl.semaphore_signal(barrier, inc=1, device_id=peer, device_id_type=MESH)

    @pl.when(reducer)
    def _():
        for t in near:
            pl.semaphore_signal(barrier, inc=1, device_id=at_near(*t), device_id_type=MESH)
        for z in range(NR, NZ):
            for i in range(NY):
                pl.semaphore_signal(barrier, inc=1, device_id=(z * NY + i, ten), device_id_type=MESH)

    def chunk(k, e):
        yy, ss = place(k, e)
        i = yy * NR + ss
        return l_hbm.at[pl.ds(pl.multiple_of((i // 4) * 16, 16), 16), pl.ds(pl.multiple_of(lax.rem(i, 4) * 128, 128), 128)]

    loads = [
        pltpu.make_async_copy(src, dst, load_sem.at[i])
        for i, (src, dst) in enumerate([(k_hbm, cot.at[c, zh, x]), (h_hbm, h), (w_hbm, w), (m_hbm, m), (v_hbm, v), (g_hbm, g), (o_hbm, o)])
    ]
    for copy in loads:
        copy.start()

    own = pltpu.make_async_copy(chunk(0, 0), raw.at[rep], load_sem.at[7])

    @pl.when(reducer)
    def _():
        own.start()

    pl.semaphore_wait(barrier, NY * NR - reducer.astype(jnp.int32) + len(peers) + zh)

    def make(src, dst, sends, recvs, i, j, device):
        return pltpu.make_async_remote_copy(
            src_ref=src, dst_ref=dst, send_sem=sends.at[i], recv_sem=recvs.at[j], device_id=device, device_id_type=MESH
        )

    mine = cot.at[c, zh, x]
    theirs = cot.at[c, 1 - zh, x]
    c_h = make(k_hbm, mine, send_c, recv_c, 0, 0, at_h)
    c_x = [make(k_hbm, mine, send_c, recv_c, k, k, at_x(k)) for k in (2, 1, 3)]
    both = [(k, other) for k in (2, 1, 3, 0) for other in (False, True) if k or other]
    c_hx = [make(theirs, theirs, send_c, recv_c, 4 + i, 4 + i, at_x(*t)) for i, t in enumerate(both)]
    row = cot.at[c, zh]
    c_c = make(row, row, send_c, recv_c, 11, 11, at_x(0, True))

    @pl.when(zh == 1)
    def _():
        c_h.start()
        pl.semaphore_signal(ready, inc=1, device_id=at_h, device_id_type=MESH)

    f_raw = [make(chunk(*t), raw.at[rep], send_r, recv_r, t[0] * NR + t[1], rep, at_near(*t)) for t in near]
    f_own = make(chunk(0, 0), raw.at[rep], send_r, recv_r, 0, rep, at_near(0, 0))
    for copy in f_raw:
        copy.start()

    @pl.when(jnp.logical_not(reducer))
    def _():
        f_own.start()

    for copy in c_x:
        copy.start()
    loads[0].wait()
    for copy in c_x:
        copy.wait_recv()
    c_c.start()

    f_whole = [make(whole.at[me], whole.at[me], send_w, recv_w, t[0] * NR + t[1], t[0] * NR + t[1], at_near(*t)) for t in near]
    f_z = [make(whole.at[me], whole.at[me], send_z, recv_z, z, side, (z * NY + y, ten)) for z in range(NR, NZ)]

    @pl.when(reducer)
    def _():
        own.wait()

        def plane(z, total):
            for i in range(NY):
                slot = z * NY + i

                @pl.when(slot != rep)
                def _():
                    make(raw.at[slot], raw.at[slot], send_r, recv_r, 0, slot, at_near(0, 1)).wait_recv()

            for i in range(NY):
                total += raw[z * NY + i].astype(F32)
            return total

        whole[me] = lax.fori_loop(0, NZ, plane, jnp.zeros((16, 128), F32))
        for copy in f_whole:
            copy.start()
        for copy in f_z:
            copy.start()

    @pl.when(zh == 0)
    def _():
        pl.semaphore_wait(ready, 1)
        c_h.start()

    c_h.wait_recv()
    for copy in c_hx:
        copy.start()

    both_chunks = whole.at[pl.ds(y * NR, NR)]
    f_y = [make(both_chunks, both_chunks, send_y, recv_y, k, k, at_y(k)) for k in (4, 3, 5, 2, 6, 1, 7)]

    @pl.when(jnp.logical_not(reducer))
    def _():
        for i in range(NR):
            slot = whole.at[y * NR + i]
            make(slot, slot, send_z, recv_z, 0, i, at_near(0, 0)).wait_recv()
        for copy in f_y:
            copy.start()

    for copy in loads[1:5]:
        copy.wait()
    c_c.wait_recv()
    for copy in c_hx:
        copy.wait_recv()
    keys = jnp.concatenate([cot[k, i, j] for i in range(NH) for j in range(NX) for k in range(NC)], axis=0)
    for i in range(4):
        rows = slice(i * 128, i * 128 + 128)
        grad = lax.dot_general(h[:, rows], keys, (((0,), (0,)), ((), ())), preferred_element_type=F32)
        first = beta_one * m[rows].astype(F32) + (1.0 - beta_one) * grad
        second = beta_two * v[rows].astype(F32) + (1.0 - beta_two) * grad * grad
        weight = w[rows].astype(F32)
        update = first / corr_one / (jnp.sqrt(second / corr_two) + adam_eps) + decay_rate * weight
        nw_ref[rows] = (weight - inner_rate * update).astype(BF16)
        nm_ref[rows] = first.astype(BF16)
        nv_ref[rows] = second.astype(BF16)

    for copy in loads[5:]:
        copy.wait()

    @pl.when(reducer)
    def _():
        for copy in f_whole:
            copy.wait_recv()

    @pl.when(jnp.logical_not(reducer))
    def _():
        for copy in f_y:
            copy.wait_recv()

    for i in range(NR * NY):
        r, q = (i // 4) * 16, (i % 4) * 128
        area = (slice(r, r + 16), slice(q, q + 128))
        delta = g[area] - whole[i] * (1.0 / (NY * NZ))
        fresh = outer_mu * o[area] + delta
        no_ref[area] = fresh
        ng_ref[area] = g[area] - outer_rate * (delta + outer_mu * fresh)

    for copy in [c_h, c_c] + c_x + c_hx + f_raw:
        copy.wait_send()

    @pl.when(reducer)
    def _():
        for copy in f_whole + f_z:
            copy.wait_send()

    @pl.when(jnp.logical_not(reducer))
    def _():
        for copy in [f_own] + f_y:
            copy.wait_send()


def store_kernel(*refs):
    sems = refs[10]
    copies = [pltpu.make_async_copy(refs[i], refs[5 + i], sems.at[i]) for i in range(5)]
    for copy in copies:
        copy.start()
    for copy in copies:
        copy.wait()


def per_device(hidden, cotangent, weight, first, second, local, glob, momentum):
    hidden, cotangent, weight, first, second, local = (a[0] for a in (hidden, cotangent, weight, first, second, local))
    args = (hidden, cotangent, weight, first, second, local, glob, momentum)
    (tok, d), (ktok, kv), (rows, _) = hidden.shape, cotangent.shape, glob.shape
    vm = pl.BlockSpec(memory_space=pltpu.VMEM)
    out = pl.pallas_call(
        kernel,
        out_shape=[
            jax.ShapeDtypeStruct((d, kv), BF16),
            jax.ShapeDtypeStruct((d, kv), BF16),
            jax.ShapeDtypeStruct((d, kv), BF16),
            jax.ShapeDtypeStruct((rows, kv), F32),
            jax.ShapeDtypeStruct((rows, kv), F32),
        ],
        in_specs=[pl.BlockSpec(memory_space=pltpu.HBM)] * 8,
        out_specs=[vm] * 5,
        scratch_shapes=[
            pltpu.VMEM((tok, d), BF16),
            pltpu.VMEM((d, kv), BF16),
            pltpu.VMEM((d, kv), BF16),
            pltpu.VMEM((d, kv), BF16),
            pltpu.VMEM((rows, kv), F32),
            pltpu.VMEM((rows, kv), F32),
            pltpu.VMEM((NC, NH, NX, ktok, kv), BF16),
            pltpu.VMEM((NY * NZ, 16, 128), BF16),
            pltpu.VMEM((NR * NY, 16, 128), F32),
            pltpu.SemaphoreType.DMA((8,)),
            pltpu.SemaphoreType.DMA((12,)),
            pltpu.SemaphoreType.DMA((12,)),
            pltpu.SemaphoreType.DMA((16,)),
            pltpu.SemaphoreType.DMA((NY * NZ,)),
            pltpu.SemaphoreType.DMA((16,)),
            pltpu.SemaphoreType.DMA((16,)),
            pltpu.SemaphoreType.DMA((NZ,)),
            pltpu.SemaphoreType.DMA((NR,)),
            pltpu.SemaphoreType.DMA((NY,)),
            pltpu.SemaphoreType.DMA((NY,)),
            pltpu.SemaphoreType.REGULAR,
        ],
        compiler_params=pltpu.CompilerParams(
            collective_id=0, has_side_effects=True, vmem_limit_bytes=16 * 1024 * 1024
        ),
    )(*(pltpu.with_memory_space_constraint(a, pltpu.HBM) for a in args))
    out = pl.pallas_call(
        store_kernel,
        out_shape=[jax.ShapeDtypeStruct(a.shape, a.dtype) for a in out],
        in_specs=[vm] * 5,
        out_specs=[pl.BlockSpec(memory_space=pltpu.HBM)] * 5,
        scratch_shapes=[pltpu.SemaphoreType.DMA((5,))],
        compiler_params=pltpu.CompilerParams(vmem_limit_bytes=4 * 1024 * 1024),
    )(*out)
    return (out[0][None], out[1][None], out[2][None], out[3], out[4])


def solution(mesh):
    return jax.shard_map(
        per_device,
        mesh=mesh,
        in_specs=(
            P("replica", None, "tensor"),
            P("replica", "tensor", None),
            P("replica", "tensor", None),
            P("replica", "tensor", None),
            P("replica", "tensor", None),
            P("replica", "tensor", None),
            P("tensor", None),
            P("tensor", None),
        ),
        out_specs=(
            P("replica", "tensor", None),
            P("replica", "tensor", None),
            P("replica", "tensor", None),
            P("tensor", None),
            P("tensor", None),
        ),
        check_vma=False,
    )
```

```python
import jax
import jax.numpy as jnp
from jax import lax
from jax.experimental import pallas as pl
from jax.experimental.pallas import tpu as pltpu
from jax.sharding import PartitionSpec as P

ADAM_STEP = 4
beta_one = 0.9
beta_two = 0.95
adam_eps = 1e-08
inner_rate = 0.01
decay_rate = 0.1
outer_rate = 0.7
outer_mu = 0.9
corr_one = 1.0 - beta_one**ADAM_STEP
corr_two = 1.0 - beta_two**ADAM_STEP

MESH = pl.DeviceIdType.MESH
NY, NZ, NX, NH, NC = 8, 8, 4, 2, 2
NR = 2
HUB = 4
F32 = jnp.float32
BF16 = jnp.bfloat16


def kernel(
    h_hbm, k_hbm, w_hbm, m_hbm, v_hbm, l_hbm, g_hbm, o_hbm,
    nw_ref, nm_ref, nv_ref, ng_ref, no_ref,
    h, w, m, v, g, o, cot, raw, part, sums, whole,
    load_sem, send_c, recv_c, send_r, recv_r, send_w, recv_w, send_z, recv_z, send_y, recv_y, send_s, recv_s, send_d, recv_d, ready, go,
):
    rep, ten = lax.axis_index("replica"), lax.axis_index("tensor")
    zl, y = rep // NY, lax.rem(rep, NY)
    zh, x, c = ten // (NX * NC), lax.rem(ten // NC, NX), lax.rem(ten, NC)
    upper = zh == 1
    lower = zh == 0
    pair = zl // 2
    low = jnp.where(upper, pair * 2, jnp.where(ten == 0, 1, 0))
    side = zl - low
    inside = jnp.logical_and(side >= 0, side < NR)
    reducer = jnp.logical_and(lower, inside)
    plain = jnp.logical_and(lower, jnp.logical_not(inside))
    direct = jnp.logical_and(lower, side < 0)
    column = jnp.logical_and(lower, side >= NR)
    side = lax.rem(zl + jnp.where(upper, 0, low), NR)
    me = y * NR + side
    quick = jnp.logical_and(upper, zl < HUB)
    hub = jnp.logical_and(upper, pair == HUB // 2)
    last = jnp.logical_and(upper, pair == HUB // 2 + 1)
    greets = jnp.logical_or(upper, zl < NR + 1)
    first_plain = 3

    near = sorted(((k, e) for k in range(NY) for e in range(NR) if k + e > 0), key=lambda t: -(min(t[0], NY - t[0]) + t[1]))

    def place(k, e):
        return lax.rem(y + k, NY), (1 - side if e else side)

    def at_near(k, e):
        yy, ss = place(k, e)
        return ((low + ss) * NY + yy, ten)

    def at_y(k):
        return (zl * NY + lax.rem(y + k, NY), ten)

    def at_x(k, other=False, half=zh):
        return (rep, half * NX * NC + lax.rem(x + k, NX) * NC + (1 - c if other else c))

    def at_pair(k):
        return ((lax.rem(pair + k, NZ // 2) * 2 + side) * NY + y, ten)

    def at_z(z):
        return (jnp.where(z < low, z, z + NR) * NY + y, ten)

    at_h = (rep, (1 - zh) * NX * NC + x * NC + c)

    barrier = pltpu.get_barrier_semaphore()

    everyone = [(k, other) for k in (2, 1, 3, 0) for other in (False, True)]
    peers = [t for t in everyone if t != (0, False)]

    def tell(device, sem=barrier):
        pl.semaphore_signal(sem, inc=1, device_id=device, device_id_type=MESH)

    @pl.when(lower)
    def _():
        tell(at_h)

    @pl.when(jnp.logical_and(lower, zl >= NR + 1))
    def _():
        for t in peers:
            tell(at_x(*t, half=1))

    @pl.when(quick)
    def _():
        for z in (HUB, HUB + 1):
            for i in range(NY):
                tell((z * NY + i, ten))
        tell(((HUB + 2 + side) * NY + y, ten))

    @pl.when(hub)
    def _():
        tell(((HUB + 2 + side) * NY + y, ten))

    @pl.when(last)
    def _():
        tell(((HUB + side) * NY + y, ten))

    @pl.when(jnp.logical_or(hub, last))
    def _():
        for t in near:
            tell(at_near(*t))

    @pl.when(greets)
    def _():
        for t in peers:
            tell(at_x(*t))

    @pl.when(reducer)
    def _():
        for z in range(NZ - NR - 1, -1, -1):
            for i in range(NY):
                there = jnp.where(z < low, z, z + NR)
                tell((there * NY + i, ten))

    def chunk(k, e):
        yy, ss = place(k, e)
        i = yy * NR + ss
        return l_hbm.at[pl.ds(pl.multiple_of((i // 4) * 16, 16), 16), pl.ds(pl.multiple_of(lax.rem(i, 4) * 128, 128), 128)]

    loads = [
        pltpu.make_async_copy(src, dst, load_sem.at[i])
        for i, (src, dst) in enumerate([(k_hbm, cot.at[c, zh, x]), (h_hbm, h), (w_hbm, w), (m_hbm, m), (v_hbm, v), (g_hbm, g), (o_hbm, o)])
    ]
    own = pltpu.make_async_copy(chunk(0, 0), raw.at[rep], load_sem.at[7])

    waits = (
        jnp.where(plain, NR * NY, 0)
        + jnp.where(greets, len(peers), 0)
        + jnp.where(upper, jnp.where(zl < NR + 1, 1, len(everyone)), 0)
        + jnp.where(hub, len(near) + HUB * NY + 1, 0)
        + jnp.where(last, len(near) + NZ // 2 - 1, 0)
    )
    pl.semaphore_wait(barrier, waits)

    def make(src, dst, sends, recvs, i, j, device):
        return pltpu.make_async_remote_copy(
            src_ref=src, dst_ref=dst, send_sem=sends.at[i], recv_sem=recvs.at[j], device_id=device, device_id_type=MESH
        )

    mine = cot.at[c, zh, x]
    theirs = cot.at[c, 1 - zh, x]
    c_h = make(k_hbm, mine, send_c, recv_c, 0, 0, at_h)
    c_x = [make(k_hbm, mine, send_c, recv_c, k, k, at_x(k)) for k in (2, 1, 3)]
    c_hx = [make(theirs, theirs, send_c, recv_c, 4 + i, 4 + i, at_x(*t)) for i, t in enumerate(peers)]
    row = cot.at[c, zh]
    c_c = make(row, row, send_c, recv_c, 11, 11, at_x(0, True))

    f_raw = [make(chunk(*t), raw.at[rep], send_r, recv_r, t[0] * NR + t[1], rep, at_near(*t)) for t in near]
    f_own = make(chunk(0, 0), raw.at[rep], send_r, recv_r, 0, rep, at_near(0, 0))

    @pl.when(upper)
    def _():
        c_h.start()
        tell(at_h, ready)

    @pl.when(hub)
    def _():
        for z in range(0, HUB, NR):
            tell(((z + side) * NY + y, ten), go)

    @pl.when(jnp.logical_or(plain, jnp.logical_or(hub, last)))
    def _():
        for copy in f_raw:
            copy.start()

    @pl.when(plain)
    def _():
        f_own.start()

    for copy in loads:
        copy.start()

    @pl.when(upper)
    def _():
        own.start()
        for copy in c_x:
            copy.start()

    @pl.when(quick)
    def _():
        pl.semaphore_wait(go, 1)
        for copy in f_raw:
            copy.start()

    f_whole = [make(whole.at[me], whole.at[me], send_w, recv_w, t[0] * NR + t[1], t[0] * NR + t[1], at_near(*t)) for t in near]
    f_z = [make(whole.at[me], whole.at[me], send_z, recv_z, z, side, at_z(z)) for z in range(NZ - NR)]

    f_sum = [make(part, sums.at[pair], send_s, recv_s, k - 1, k - 1, at_pair(k)) for k in range(1, NZ // 2)]
    f_direct = [make(whole.at[me], whole.at[me], send_d, recv_d, k, me, (lax.rem(y + k, NY), ten)) for k in (4, 3, 5, 2, 6, 1, 7, 0)]

    def arrived(slot):
        make(raw.at[slot], raw.at[slot], send_r, recv_r, 0, slot, at_y(1)).wait_recv()

    @pl.when(reducer)
    def _():
        own.start()
        arrived(first_plain * NY + y)
        for copy in f_raw:
            copy.start()
        own.wait()

        def plane(i, total):
            z = jnp.where(i < 4, i + 3, jnp.where(i < 7, i - 4, 7))
            for j in range(NY):
                slot = z * NY + j

                @pl.when(jnp.logical_and(slot != rep, slot != first_plain * NY + y))
                def _():
                    arrived(slot)

            for j in range(NY):
                total += raw[z * NY + j].astype(F32)
            return total

        whole[me] = lax.fori_loop(0, NZ, plane, jnp.zeros((16, 128), F32))
        for copy in f_whole:
            copy.start()

        @pl.when(low == 0)
        def _():
            f_z[0].start()

        @pl.when(low == 1)
        def _():
            for copy in f_direct:
                copy.start()

        for copy in f_z[1:]:
            copy.start()

    @pl.when(upper)
    def _():
        own.wait()
        total = jnp.zeros((16, 128), F32)
        for e in range(NR):
            for j in range(NY):
                slot = (low + e) * NY + j

                @pl.when(slot != rep)
                def _():
                    arrived(slot)

                total += raw[slot].astype(F32)
        part[...] = total
        for copy in f_sum:
            copy.start()
        sums[pair] = total

    @pl.when(lower)
    def _():
        pl.semaphore_wait(ready, 1)
        c_h.start()
        for copy in c_x:
            copy.start()

    c_h.wait_recv()
    for copy in c_hx:
        copy.start()
    loads[0].wait()
    for copy in c_x:
        copy.wait_recv()
    c_c.start()

    both_chunks = whole.at[pl.ds(y * NR, NR)]
    f_y = [make(both_chunks, both_chunks, send_y, recv_y, k, k, at_y(k)) for k in (4, 3, 5, 2, 6, 1, 7)]

    @pl.when(column)
    def _():
        for i in range(NR):
            slot = whole.at[y * NR + i]
            make(slot, slot, send_z, recv_z, 0, i, at_y(1)).wait_recv()
        for copy in f_y:
            copy.start()

    @pl.when(upper)
    def _():
        for copy in f_sum:
            copy.wait_recv()
        total = sums[0]
        for i in range(1, NZ // 2):
            total += sums[i]
        whole[me] = total
        for copy in f_whole:
            copy.start()

    for copy in loads[1:5]:
        copy.wait()
    c_c.wait_recv()
    for copy in c_hx:
        copy.wait_recv()
    keys = jnp.concatenate([cot[k, i, j] for i in range(NH) for j in range(NX) for k in range(NC)], axis=0)
    for i in range(4):
        rows = slice(i * 128, i * 128 + 128)
        grad = lax.dot_general(h[:, rows], keys, (((0,), (0,)), ((), ())), preferred_element_type=F32)
        first = beta_one * m[rows].astype(F32) + (1.0 - beta_one) * grad
        second = beta_two * v[rows].astype(F32) + (1.0 - beta_two) * grad * grad
        scaled = second * (1.0 / corr_two)
        root = scaled * lax.rsqrt(scaled)
        step = first * (inner_rate / corr_one) / (root + adam_eps)
        nw_ref[rows] = (w[rows].astype(F32) * (1.0 - inner_rate * decay_rate) - step).astype(BF16)
        nm_ref[rows] = first.astype(BF16)
        nv_ref[rows] = second.astype(BF16)

    for copy in loads[5:]:
        copy.wait()

    @pl.when(inside)
    def _():
        for copy in f_whole:
            copy.wait_recv()

    @pl.when(column)
    def _():
        for copy in f_y:
            copy.wait_recv()

    @pl.when(direct)
    def _():
        for i in range(NR * NY):
            make(whole.at[i], whole.at[i], send_d, recv_d, 0, i, at_y(1)).wait_recv()

    for i in range(NR * NY):
        r, q = (i // 4) * 16, (i % 4) * 128
        area = (slice(r, r + 16), slice(q, q + 128))
        delta = g[area] - whole[i] * (1.0 / (NY * NZ))
        fresh = outer_mu * o[area] + delta
        no_ref[area] = fresh
        ng_ref[area] = g[area] - outer_rate * (delta + outer_mu * fresh)

    for copy in [c_h, c_c] + c_x + c_hx + f_raw:
        copy.wait_send()

    @pl.when(inside)
    def _():
        for copy in f_whole:
            copy.wait_send()

    @pl.when(reducer)
    def _():
        for copy in f_z[1:]:
            copy.wait_send()

        @pl.when(low == 0)
        def _():
            f_z[0].wait_send()

        @pl.when(low == 1)
        def _():
            for copy in f_direct:
                copy.wait_send()

    @pl.when(upper)
    def _():
        for copy in f_sum:
            copy.wait_send()

    @pl.when(plain)
    def _():
        f_own.wait_send()

    @pl.when(column)
    def _():
        for copy in f_y:
            copy.wait_send()


def store_kernel(*refs):
    sems = refs[10]
    copies = [pltpu.make_async_copy(refs[i], refs[5 + i], sems.at[i]) for i in range(5)]
    for copy in copies:
        copy.start()
    for copy in copies:
        copy.wait()


def per_device(hidden, cotangent, weight, first, second, local, glob, momentum):
    hidden, cotangent, weight, first, second, local = (a[0] for a in (hidden, cotangent, weight, first, second, local))
    args = (hidden, cotangent, weight, first, second, local, glob, momentum)
    (tok, d), (ktok, kv), (rows, _) = hidden.shape, cotangent.shape, glob.shape
    vm = pl.BlockSpec(memory_space=pltpu.VMEM)
    out = pl.pallas_call(
        kernel,
        out_shape=[
            jax.ShapeDtypeStruct((d, kv), BF16),
            jax.ShapeDtypeStruct((d, kv), BF16),
            jax.ShapeDtypeStruct((d, kv), BF16),
            jax.ShapeDtypeStruct((rows, kv), F32),
            jax.ShapeDtypeStruct((rows, kv), F32),
        ],
        in_specs=[pl.BlockSpec(memory_space=pltpu.HBM)] * 8,
        out_specs=[vm] * 5,
        scratch_shapes=[
            pltpu.VMEM((tok, d), BF16),
            pltpu.VMEM((d, kv), BF16),
            pltpu.VMEM((d, kv), BF16),
            pltpu.VMEM((d, kv), BF16),
            pltpu.VMEM((rows, kv), F32),
            pltpu.VMEM((rows, kv), F32),
            pltpu.VMEM((NC, NH, NX, ktok, kv), BF16),
            pltpu.VMEM((NY * NZ, 16, 128), BF16),
            pltpu.VMEM((16, 128), F32),
            pltpu.VMEM((NZ // 2, 16, 128), F32),
            pltpu.VMEM((NR * NY, 16, 128), F32),
            pltpu.SemaphoreType.DMA((8,)),
            pltpu.SemaphoreType.DMA((12,)),
            pltpu.SemaphoreType.DMA((12,)),
            pltpu.SemaphoreType.DMA((16,)),
            pltpu.SemaphoreType.DMA((NY * NZ,)),
            pltpu.SemaphoreType.DMA((16,)),
            pltpu.SemaphoreType.DMA((16,)),
            pltpu.SemaphoreType.DMA((NZ,)),
            pltpu.SemaphoreType.DMA((NR,)),
            pltpu.SemaphoreType.DMA((NY,)),
            pltpu.SemaphoreType.DMA((NY,)),
            pltpu.SemaphoreType.DMA((3,)),
            pltpu.SemaphoreType.DMA((3,)),
            pltpu.SemaphoreType.DMA((NY,)),
            pltpu.SemaphoreType.DMA((NR * NY,)),
            pltpu.SemaphoreType.REGULAR,
            pltpu.SemaphoreType.REGULAR,
        ],
        compiler_params=pltpu.CompilerParams(
            collective_id=0, has_side_effects=True, vmem_limit_bytes=16 * 1024 * 1024
        ),
    )(*(pltpu.with_memory_space_constraint(a, pltpu.HBM) for a in args))
    out = pl.pallas_call(
        store_kernel,
        out_shape=[jax.ShapeDtypeStruct(a.shape, a.dtype) for a in out],
        in_specs=[vm] * 5,
        out_specs=[pl.BlockSpec(memory_space=pltpu.HBM)] * 5,
        scratch_shapes=[pltpu.SemaphoreType.DMA((5,))],
        compiler_params=pltpu.CompilerParams(vmem_limit_bytes=4 * 1024 * 1024),
    )(*out)
    return (out[0][None], out[1][None], out[2][None], out[3], out[4])


def solution(mesh):
    return jax.shard_map(
        per_device,
        mesh=mesh,
        in_specs=(
            P("replica", None, "tensor"),
            P("replica", "tensor", None),
            P("replica", "tensor", None),
            P("replica", "tensor", None),
            P("replica", "tensor", None),
            P("replica", "tensor", None),
            P("tensor", None),
            P("tensor", None),
        ),
        out_specs=(
            P("replica", "tensor", None),
            P("replica", "tensor", None),
            P("replica", "tensor", None),
            P("tensor", None),
            P("tensor", None),
        ),
        check_vma=False,
    )
```

```python
import jax
import jax.numpy as jnp
from jax import lax
from jax.experimental import pallas as pl
from jax.experimental.pallas import tpu as pltpu
from jax.sharding import PartitionSpec as P

ADAM_STEP = 4
beta_one = 0.9
beta_two = 0.95
adam_eps = 1e-08
inner_rate = 0.01
decay_rate = 0.1
outer_rate = 0.7
outer_mu = 0.9
corr_one = 1.0 - beta_one**ADAM_STEP
corr_two = 1.0 - beta_two**ADAM_STEP

MESH = pl.DeviceIdType.MESH
NY, NZ, NX, NH, NC = 8, 8, 4, 2, 2
NR = 2
HUB = 4
F32 = jnp.float32
BF16 = jnp.bfloat16


def kernel(
    h_hbm, k_hbm, w_hbm, m_hbm, v_hbm, l_hbm, g_hbm, o_hbm,
    nw_ref, nm_ref, nv_ref, ng_ref, no_ref,
    h, w, m, v, g, o, cot, raw, part, sums, whole,
    load_sem, send_c, recv_c, send_r, recv_r, send_w, recv_w, send_z, recv_z, send_y, recv_y, send_s, recv_s, send_d, recv_d, ready, go,
):
    rep, ten = lax.axis_index("replica"), lax.axis_index("tensor")
    zl, y = rep // NY, lax.rem(rep, NY)
    zh, x, c = ten // (NX * NC), lax.rem(ten // NC, NX), lax.rem(ten, NC)
    upper = zh == 1
    lower = zh == 0
    pair = zl // 2

    def low_of(yy):
        return jnp.where(jnp.logical_and(ten == 0, yy == 0), 1, 0)

    low = jnp.where(upper, pair * 2, low_of(y))
    side = zl - low
    inside = jnp.logical_and(side >= 0, side < NR)
    reducer = jnp.logical_and(lower, inside)
    plain = jnp.logical_and(lower, jnp.logical_not(inside))
    direct = jnp.logical_and(lower, side < 0)
    column = jnp.logical_and(lower, side >= NR)
    side = lax.rem(zl + jnp.where(upper, 0, low), NR)
    bridge = jnp.logical_and(reducer, zl == NR)
    me = y * NR + side
    quick = jnp.logical_and(upper, zl < HUB)
    hub = jnp.logical_and(upper, pair == HUB // 2)
    last = jnp.logical_and(upper, pair == HUB // 2 + 1)
    greets = jnp.logical_or(upper, zl < NR + 1)
    first_plain = 3
    row = rep == 0
    late = jnp.logical_and(row, ten == 0)
    stand = jnp.logical_and(row, ten == 1)
    far = jnp.logical_and(row, ten == NX * NC)

    near = sorted(((k, e) for k in range(NY) for e in range(NR) if k + e > 0), key=lambda t: -(min(t[0], NY - t[0]) + t[1]))

    def place(k, e):
        return lax.rem(y + k, NY), (1 - side if e else side)

    def at_near(k, e):
        yy, ss = place(k, e)
        return ((jnp.where(upper, low, low_of(yy)) + ss) * NY + yy, ten)

    def at_y(k):
        return (zl * NY + lax.rem(y + k, NY), ten)

    def at_x(k, other=False, half=zh):
        return (rep, half * NX * NC + lax.rem(x + k, NX) * NC + (1 - c if other else c))

    def at_pair(k):
        return ((lax.rem(pair + k, NZ // 2) * 2 + side) * NY + y, ten)

    def at_z(z):
        return (jnp.where(z < low, z, z + NR) * NY + y, ten)

    at_h = (rep, (1 - zh) * NX * NC + x * NC + c)

    barrier = pltpu.get_barrier_semaphore()

    everyone = [(k, other) for k in (2, 1, 3, 0) for other in (False, True)]
    peers = [t for t in everyone if t != (0, False)]

    def tell(device, sem=barrier):
        pl.semaphore_signal(sem, inc=1, device_id=device, device_id_type=MESH)

    @pl.when(reducer)
    def _():
        tell(at_h)

    @pl.when(stand)
    def _():
        tell((rep, NX * NC))

    @pl.when(quick)
    def _():
        for z in (HUB, HUB + 1):
            for i in range(NY):
                tell((z * NY + i, ten))
        tell(((HUB + 2 + side) * NY + y, ten))

    @pl.when(hub)
    def _():
        tell(((HUB + 2 + side) * NY + y, ten))

    @pl.when(last)
    def _():
        tell(((HUB + side) * NY + y, ten))

    @pl.when(jnp.logical_or(hub, last))
    def _():
        for t in near:
            tell(at_near(*t))

    @pl.when(greets)
    def _():
        for t in peers:
            tell(at_x(*t))

    @pl.when(reducer)
    def _():
        for z in range(NZ - NR - 1, -1, -1):
            for i in range(NY):
                there = jnp.where(z < low_of(i), z, z + NR)
                tell((there * NY + i, ten))

    def chunk(k, e):
        yy, ss = place(k, e)
        i = yy * NR + ss
        return l_hbm.at[pl.ds(pl.multiple_of((i // 4) * 16, 16), 16), pl.ds(pl.multiple_of(lax.rem(i, 4) * 128, 128), 128)]

    loads = [
        pltpu.make_async_copy(src, dst, load_sem.at[i])
        for i, (src, dst) in enumerate([(k_hbm, cot.at[c, zh, x]), (h_hbm, h), (w_hbm, w), (m_hbm, m), (v_hbm, v), (g_hbm, g), (o_hbm, o)])
    ]
    own = pltpu.make_async_copy(chunk(0, 0), raw.at[rep], load_sem.at[7])

    waits = (
        jnp.where(plain, NR * NY, 0)
        + jnp.where(greets, len(peers), 0)
        + jnp.where(upper, jnp.where(zl < NR + 1, 1, len(everyone)), 0)
        + jnp.where(hub, len(near) + HUB * NY + 1, 0)
        + jnp.where(last, len(near) + NZ // 2 - 1, 0)
    )
    pl.semaphore_wait(barrier, waits)

    def make(src, dst, sends, recvs, i, j, device):
        return pltpu.make_async_remote_copy(
            src_ref=src, dst_ref=dst, send_sem=sends.at[i], recv_sem=recvs.at[j], device_id=device, device_id_type=MESH
        )

    mine = cot.at[c, zh, x]
    theirs = cot.at[c, 1 - zh, x]
    c_h = make(k_hbm, mine, send_c, recv_c, 0, 0, at_h)
    c_x = [make(k_hbm, mine, send_c, recv_c, k, k, at_x(k)) for k in (2, 1, 3)]
    c_hx = [make(theirs, theirs, send_c, recv_c, 4 + i, 4 + i, at_x(*t)) for i, t in enumerate(peers)]
    half = cot.at[c, zh]
    c_c = make(half, half, send_c, recv_c, 11, 11, at_x(0, True))
    missed = cot.at[0, 1, 0]
    c_far = make(k_hbm, missed, send_c, recv_c, 0, 12, (rep, 1))
    c_stand = [
        make(missed, missed, send_c, recv_c, 13 + i, 0 if t == (0, True) else 4 + i, (rep, 0 if t == (0, True) else t[0] * NC + t[1]))
        for i, t in enumerate(peers)
    ]

    f_raw = [make(chunk(*t), raw.at[rep], send_r, recv_r, t[0] * NR + t[1], rep, at_near(*t)) for t in near]
    f_own = make(chunk(0, 0), raw.at[rep], send_r, recv_r, 0, rep, at_near(0, 0))

    @pl.when(jnp.logical_and(upper, jnp.logical_not(far)))
    def _():
        c_h.start()
        tell(at_h, ready)

    @pl.when(far)
    def _():
        c_far.start()

    @pl.when(hub)
    def _():
        for z in range(0, HUB, NR):
            tell(((z + side) * NY + y, ten), go)

    @pl.when(jnp.logical_or(plain, jnp.logical_or(hub, last)))
    def _():
        for copy in f_raw:
            copy.start()

    @pl.when(plain)
    def _():
        f_own.start()

    @pl.when(jnp.logical_and(plain, jnp.logical_not(late)))
    def _():
        tell(at_h)

    @pl.when(jnp.logical_and(lower, zl >= NR + 1))
    def _():
        for t in peers:
            tell(at_x(*t, half=1))

    for copy in loads:
        copy.start()

    @pl.when(upper)
    def _():
        own.start()

    @pl.when(greets)
    def _():
        for copy in c_x:
            copy.start()

    @pl.when(quick)
    def _():
        pl.semaphore_wait(go, 1)
        for copy in f_raw:
            copy.start()

    f_whole = [make(whole.at[me], whole.at[me], send_w, recv_w, t[0] * NR + t[1], t[0] * NR + t[1], at_near(*t)) for t in near]
    f_z = [make(whole.at[me], whole.at[me], send_z, recv_z, z, side, at_z(z)) for z in range(NZ - NR)]

    f_sum = [make(part, sums.at[pair], send_s, recv_s, k - 1, k - 1, at_pair(k)) for k in range(1, NZ // 2)]
    f_direct = [make(whole.at[me], whole.at[me], send_d, recv_d, k, me, (0, 0)) for k in (0,)]

    def own_half():
        loads[0].wait()
        for copy in c_x:
            copy.wait_recv()
        c_c.start()

    def arrived(slot):
        make(raw.at[slot], raw.at[slot], send_r, recv_r, 0, slot, at_y(1)).wait_recv()

    @pl.when(reducer)
    def _():
        own.start()
        arrived(first_plain * NY + y)
        for copy in f_raw:
            copy.start()
        own_half()
        own.wait()

        def plane(i, total):
            z = jnp.where(i < 4, i + 3, jnp.where(i < 7, i - 4, 7))
            for j in range(NY):
                slot = z * NY + j

                @pl.when(jnp.logical_and(slot != rep, slot != first_plain * NY + y))
                def _():
                    arrived(slot)

            for j in range(NY):
                total += raw[z * NY + j].astype(F32)
            return total

        whole[me] = lax.fori_loop(0, NZ, plane, jnp.zeros((16, 128), F32))
        for copy in f_whole[:7]:
            copy.start()

        @pl.when(low == 0)
        def _():
            f_z[0].start()

        @pl.when(ten == 0)
        def _():
            for copy in f_direct:
                copy.start()

        for copy in f_z[1:] + f_whole[7:]:
            copy.start()

    @pl.when(upper)
    def _():
        own.wait()
        total = jnp.zeros((16, 128), F32)
        for e in range(NR):
            for j in range(NY):
                slot = (low + e) * NY + j

                @pl.when(slot != rep)
                def _():
                    arrived(slot)

                total += raw[slot].astype(F32)
        part[...] = total
        for copy in f_sum:
            copy.start()
        sums[pair] = total

    @pl.when(jnp.logical_and(lower, jnp.logical_not(late)))
    def _():
        pl.semaphore_wait(ready, 1)
        c_h.start()

    @pl.when(jnp.logical_not(greets))
    def _():
        for copy in c_x:
            copy.start()

    chunks = whole.at[pl.ds(y * NR, NR)]
    f_y = [make(chunks, chunks, send_y, recv_y, k, k, at_y(k)) for k in (4, 3, 5, 2, 6, 1, 7)]
    f_skip = [jnp.logical_and(jnp.logical_and(ten == 0, zl == NR), lax.rem(y + k, NY) == 0) for k in (4, 3, 5, 2, 6, 1, 7)]

    def along_y():
        for i in range(NR):
            slot = whole.at[y * NR + i]
            make(slot, slot, send_z, recv_z, 0, i, at_y(1)).wait_recv()
        for skip, copy in zip(f_skip, f_y):

            @pl.when(jnp.logical_not(skip))
            def _():
                copy.start()

    @pl.when(jnp.logical_and(column, zl >= HUB))
    def _():
        along_y()

    c_h.wait_recv()

    @pl.when(late)
    def _():
        c_h.start()

    @pl.when(jnp.logical_not(late))
    def _():
        for copy in c_hx:
            copy.start()

    @pl.when(stand)
    def _():
        c_far.wait_recv()
        for copy in c_stand:
            copy.start()

    @pl.when(jnp.logical_and(column, zl < HUB))
    def _():
        along_y()

    @pl.when(jnp.logical_not(reducer))
    def _():
        own_half()

    f_next = f_whole[near.index((0, 1))]

    @pl.when(bridge)
    def _():
        f_next.wait_recv()
        for copy in f_y:
            copy.start()

    @pl.when(upper)
    def _():
        for copy in f_sum:
            copy.wait_recv()
        total = sums[0]
        for i in range(1, NZ // 2):
            total += sums[i]
        whole[me] = total
        for copy in f_whole:
            copy.start()

    for copy in loads[1:5]:
        copy.wait()
    c_c.wait_recv()
    for t, copy in zip(peers, c_hx):
        if t == (0, True):

            @pl.when(jnp.logical_not(stand))
            def _():
                copy.wait_recv()

        else:
            copy.wait_recv()
    keys = jnp.concatenate([cot[k, i, j] for i in range(NH) for j in range(NX) for k in range(NC)], axis=0)
    for i in range(4):
        rows = slice(i * 128, i * 128 + 128)
        grad = lax.dot_general(h[:, rows], keys, (((0,), (0,)), ((), ())), preferred_element_type=F32)
        first = beta_one * m[rows].astype(F32) + (1.0 - beta_one) * grad
        second = beta_two * v[rows].astype(F32) + (1.0 - beta_two) * grad * grad
        scaled = second * (1.0 / corr_two)
        root = scaled * lax.rsqrt(scaled)
        step = first * (inner_rate / corr_one) / (root + adam_eps)
        nw_ref[rows] = (w[rows].astype(F32) * (1.0 - inner_rate * decay_rate) - step).astype(BF16)
        nm_ref[rows] = first.astype(BF16)
        nv_ref[rows] = second.astype(BF16)

    for copy in [c_h, c_c] + c_x + f_raw:
        copy.wait_send()

    @pl.when(jnp.logical_not(late))
    def _():
        for copy in c_hx:
            copy.wait_send()

    @pl.when(stand)
    def _():
        for copy in c_stand:
            copy.wait_send()

    @pl.when(plain)
    def _():
        f_own.wait_send()

    @pl.when(inside)
    def _():
        for copy in f_whole:
            copy.wait_send()

    @pl.when(reducer)
    def _():
        for copy in f_z[1:]:
            copy.wait_send()

        @pl.when(low == 0)
        def _():
            f_z[0].wait_send()

        @pl.when(ten == 0)
        def _():
            for copy in f_direct:
                copy.wait_send()

    @pl.when(upper)
    def _():
        for copy in f_sum:
            copy.wait_send()

    @pl.when(column)
    def _():
        for skip, copy in zip(f_skip, f_y):

            @pl.when(jnp.logical_not(skip))
            def _():
                copy.wait_send()

    @pl.when(bridge)
    def _():
        for copy in f_y:
            copy.wait_send()

    for copy in loads[5:]:
        copy.wait()

    @pl.when(inside)
    def _():
        for copy in f_whole:
            if copy is not f_next:
                copy.wait_recv()

    @pl.when(jnp.logical_and(inside, jnp.logical_not(bridge)))
    def _():
        f_next.wait_recv()

    @pl.when(column)
    def _():
        for copy in f_y:
            copy.wait_recv()

    @pl.when(direct)
    def _():
        for i in range(NR * NY):
            make(whole.at[i], whole.at[i], send_d, recv_d, 0, i, at_y(1)).wait_recv()

    for i in range(NR * NY):
        r, q = (i // 4) * 16, (i % 4) * 128
        area = (slice(r, r + 16), slice(q, q + 128))
        delta = g[area] - whole[i] * (1.0 / (NY * NZ))
        fresh = outer_mu * o[area] + delta
        no_ref[area] = fresh
        ng_ref[area] = g[area] - outer_rate * (delta + outer_mu * fresh)


def store_kernel(*refs):
    sems = refs[10]
    copies = [pltpu.make_async_copy(refs[i], refs[5 + i], sems.at[i]) for i in range(5)]
    for copy in copies:
        copy.start()
    for copy in copies:
        copy.wait()


def per_device(hidden, cotangent, weight, first, second, local, glob, momentum):
    hidden, cotangent, weight, first, second, local = (a[0] for a in (hidden, cotangent, weight, first, second, local))
    args = (hidden, cotangent, weight, first, second, local, glob, momentum)
    (tok, d), (ktok, kv), (rows, _) = hidden.shape, cotangent.shape, glob.shape
    vm = pl.BlockSpec(memory_space=pltpu.VMEM)
    out = pl.pallas_call(
        kernel,
        out_shape=[
            jax.ShapeDtypeStruct((d, kv), BF16),
            jax.ShapeDtypeStruct((d, kv), BF16),
            jax.ShapeDtypeStruct((d, kv), BF16),
            jax.ShapeDtypeStruct((rows, kv), F32),
            jax.ShapeDtypeStruct((rows, kv), F32),
        ],
        in_specs=[pl.BlockSpec(memory_space=pltpu.HBM)] * 8,
        out_specs=[vm] * 5,
        scratch_shapes=[
            pltpu.VMEM((tok, d), BF16),
            pltpu.VMEM((d, kv), BF16),
            pltpu.VMEM((d, kv), BF16),
            pltpu.VMEM((d, kv), BF16),
            pltpu.VMEM((rows, kv), F32),
            pltpu.VMEM((rows, kv), F32),
            pltpu.VMEM((NC, NH, NX, ktok, kv), BF16),
            pltpu.VMEM((NY * NZ, 16, 128), BF16),
            pltpu.VMEM((16, 128), F32),
            pltpu.VMEM((NZ // 2, 16, 128), F32),
            pltpu.VMEM((NR * NY, 16, 128), F32),
            pltpu.SemaphoreType.DMA((8,)),
            pltpu.SemaphoreType.DMA((20,)),
            pltpu.SemaphoreType.DMA((13,)),
            pltpu.SemaphoreType.DMA((16,)),
            pltpu.SemaphoreType.DMA((NY * NZ,)),
            pltpu.SemaphoreType.DMA((16,)),
            pltpu.SemaphoreType.DMA((16,)),
            pltpu.SemaphoreType.DMA((NZ,)),
            pltpu.SemaphoreType.DMA((NR,)),
            pltpu.SemaphoreType.DMA((NY,)),
            pltpu.SemaphoreType.DMA((NY,)),
            pltpu.SemaphoreType.DMA((3,)),
            pltpu.SemaphoreType.DMA((3,)),
            pltpu.SemaphoreType.DMA((1,)),
            pltpu.SemaphoreType.DMA((NR * NY,)),
            pltpu.SemaphoreType.REGULAR,
            pltpu.SemaphoreType.REGULAR,
        ],
        compiler_params=pltpu.CompilerParams(
            collective_id=0, has_side_effects=True, vmem_limit_bytes=16 * 1024 * 1024
        ),
    )(*(pltpu.with_memory_space_constraint(a, pltpu.HBM) for a in args))
    out = pl.pallas_call(
        store_kernel,
        out_shape=[jax.ShapeDtypeStruct(a.shape, a.dtype) for a in out],
        in_specs=[vm] * 5,
        out_specs=[pl.BlockSpec(memory_space=pltpu.HBM)] * 5,
        scratch_shapes=[pltpu.SemaphoreType.DMA((5,))],
        compiler_params=pltpu.CompilerParams(vmem_limit_bytes=4 * 1024 * 1024),
    )(*out)
    return (out[0][None], out[1][None], out[2][None], out[3], out[4])


def solution(mesh):
    return jax.shard_map(
        per_device,
        mesh=mesh,
        in_specs=(
            P("replica", None, "tensor"),
            P("replica", "tensor", None),
            P("replica", "tensor", None),
            P("replica", "tensor", None),
            P("replica", "tensor", None),
            P("replica", "tensor", None),
            P("tensor", None),
            P("tensor", None),
        ),
        out_specs=(
            P("replica", "tensor", None),
            P("replica", "tensor", None),
            P("replica", "tensor", None),
            P("tensor", None),
            P("tensor", None),
        ),
        check_vma=False,
    )
```

```python
import jax
import jax.numpy as jnp
from jax import lax
from jax.experimental import pallas as pl
from jax.experimental.pallas import tpu as pltpu
from jax.sharding import PartitionSpec as P

ADAM_STEP = 4
beta_one = 0.9
beta_two = 0.95
adam_eps = 1e-08
inner_rate = 0.01
decay_rate = 0.1
outer_rate = 0.7
outer_mu = 0.9
corr_one = 1.0 - beta_one**ADAM_STEP
corr_two = 1.0 - beta_two**ADAM_STEP

MESH = pl.DeviceIdType.MESH
NY, NZ, NX, NH, NC = 8, 8, 4, 2, 2
NR = 2
HUB = 4
F32 = jnp.float32
BF16 = jnp.bfloat16


def kernel(
    h_hbm, k_hbm, w_hbm, m_hbm, v_hbm, l_hbm, g_hbm, o_hbm,
    nw_ref, nm_ref, nv_ref, ng_ref, no_ref,
    h, w, m, v, g, o, cot, raw, part, sums, whole,
    load_sem, send_c, recv_c, send_r, recv_r, send_w, recv_w, send_z, recv_z, send_y, recv_y, send_s, recv_s, send_d, recv_d, ready, go,
):
    rep, ten = lax.axis_index("replica"), lax.axis_index("tensor")
    zl, y = rep // NY, lax.rem(rep, NY)
    zh, x, c = ten // (NX * NC), lax.rem(ten // NC, NX), lax.rem(ten, NC)
    upper = zh == 1
    lower = zh == 0
    pair = zl // 2

    def low_of(yy):
        return jnp.where(jnp.logical_and(ten == 0, yy == 0), 1, 0)

    low = jnp.where(upper, pair * 2, low_of(y))
    side = zl - low
    inside = jnp.logical_and(side >= 0, side < NR)
    reducer = jnp.logical_and(lower, inside)
    plain = jnp.logical_and(lower, jnp.logical_not(inside))
    direct = jnp.logical_and(lower, side < 0)
    column = jnp.logical_and(lower, side >= NR)
    side = lax.rem(zl + jnp.where(upper, 0, low), NR)
    bridge = jnp.logical_and(reducer, zl == NR)
    me = y * NR + side
    quick = jnp.logical_and(upper, zl < HUB)
    hub = jnp.logical_and(upper, pair == HUB // 2)
    last = jnp.logical_and(upper, pair == HUB // 2 + 1)
    greets = jnp.logical_or(upper, zl < NR + 1)
    first_plain = 3
    row = rep == 0
    late = jnp.logical_and(row, ten == 0)
    stand = jnp.logical_and(row, ten == 1)
    far = jnp.logical_and(row, ten == NX * NC)

    near = sorted(((k, e) for k in range(NY) for e in range(NR) if k + e > 0), key=lambda t: -(min(t[0], NY - t[0]) + t[1]))

    def place(k, e):
        return lax.rem(y + k, NY), (1 - side if e else side)

    def at_near(k, e):
        yy, ss = place(k, e)
        return ((jnp.where(upper, low, low_of(yy)) + ss) * NY + yy, ten)

    def at_y(k):
        return (zl * NY + lax.rem(y + k, NY), ten)

    def at_x(k, other=False, half=zh):
        return (rep, half * NX * NC + lax.rem(x + k, NX) * NC + (1 - c if other else c))

    def at_pair(k):
        return ((lax.rem(pair + k, NZ // 2) * 2 + side) * NY + y, ten)

    def at_z(z):
        return (jnp.where(z < low, z, z + NR) * NY + y, ten)

    at_h = (rep, (1 - zh) * NX * NC + x * NC + c)

    barrier = pltpu.get_barrier_semaphore()

    everyone = [(k, other) for k in (2, 1, 3, 0) for other in (False, True)]
    peers = [t for t in everyone if t != (0, False)]

    def tell(device, sem=barrier):
        pl.semaphore_signal(sem, inc=1, device_id=device, device_id_type=MESH)

    @pl.when(reducer)
    def _():
        tell(at_h)

    @pl.when(stand)
    def _():
        tell((rep, NX * NC))

    @pl.when(quick)
    def _():
        for z in (HUB, HUB + 1):
            for i in range(NY):
                tell((z * NY + i, ten))
        tell(((HUB + 2 + side) * NY + y, ten))

    @pl.when(hub)
    def _():
        tell(((HUB + 2 + side) * NY + y, ten))

    @pl.when(last)
    def _():
        tell(((HUB + side) * NY + y, ten))

    @pl.when(jnp.logical_or(hub, last))
    def _():
        for t in near:
            tell(at_near(*t))

    @pl.when(greets)
    def _():
        for t in peers:
            tell(at_x(*t))

    @pl.when(reducer)
    def _():
        for z in range(NZ - NR - 1, -1, -1):
            for i in range(NY):
                there = jnp.where(z < low_of(i), z, z + NR)
                tell((there * NY + i, ten))

    def chunk(k, e):
        yy, ss = place(k, e)
        i = yy * NR + ss
        return l_hbm.at[pl.ds(pl.multiple_of((i // 4) * 16, 16), 16), pl.ds(pl.multiple_of(lax.rem(i, 4) * 128, 128), 128)]

    loads = [
        pltpu.make_async_copy(src, dst, load_sem.at[i])
        for i, (src, dst) in enumerate([(k_hbm, cot.at[(c * NH + zh) * NX + x]), (h_hbm, h), (w_hbm, w), (m_hbm, m), (v_hbm, v), (g_hbm, g), (o_hbm, o)])
    ]
    own = pltpu.make_async_copy(chunk(0, 0), raw.at[rep], recv_r.at[zl])

    waits = (
        jnp.where(plain, NR * NY, 0)
        + jnp.where(greets, len(peers), 0)
        + jnp.where(upper, jnp.where(zl < NR + 1, 1, len(everyone)), 0)
        + jnp.where(hub, len(near) + HUB * NY + 1, 0)
        + jnp.where(last, len(near) + NZ // 2 - 1, 0)
    )
    pl.semaphore_wait(barrier, waits)

    def make(src, dst, sends, recvs, i, j, device):
        return pltpu.make_async_remote_copy(
            src_ref=src, dst_ref=dst, send_sem=sends.at[i], recv_sem=recvs.at[j], device_id=device, device_id_type=MESH
        )

    def blocks(n, i):
        return make(cot.at[pl.ds(0, n)], cot.at[pl.ds(0, n)], send_c, recv_c, i, i, at_h)

    mine = cot.at[(c * NH + zh) * NX + x]
    theirs = cot.at[(c * NH + 1 - zh) * NX + x]
    c_h = make(k_hbm, mine, send_c, recv_c, 0, 0, at_h)
    c_x = [make(k_hbm, mine, send_c, recv_c, 1, 1, at_x(k)) for k in (2, 1, 3)]
    c_hx = [make(theirs, theirs, send_c, recv_c, 2, 2, at_x(*t)) for t in peers]
    half = cot.at[pl.ds((c * NH + zh) * NX, NX)]
    c_c = make(half, half, send_c, recv_c, 3, 3, at_x(0, True))
    missed = cot.at[NX]
    c_far = make(k_hbm, missed, send_c, recv_c, 0, 4, (rep, 1))
    c_stand = [
        make(missed, missed, send_c, recv_c, 4, 0 if t == (0, True) else 2, (rep, 0 if t == (0, True) else t[0] * NC + t[1])) for t in peers
    ]

    f_raw = [make(chunk(*t), raw.at[rep], send_r, recv_r, 0, zl, at_near(*t)) for t in near]
    f_own = make(chunk(0, 0), raw.at[rep], send_r, recv_r, 1, zl, at_near(0, 0))

    @pl.when(jnp.logical_and(upper, jnp.logical_not(far)))
    def _():
        c_h.start()
        tell(at_h, ready)

    @pl.when(far)
    def _():
        c_far.start()

    @pl.when(hub)
    def _():
        for z in range(0, HUB, NR):
            tell(((z + side) * NY + y, ten), go)

    @pl.when(jnp.logical_or(plain, jnp.logical_or(hub, last)))
    def _():
        for copy in f_raw:
            copy.start()

    @pl.when(plain)
    def _():
        f_own.start()

    @pl.when(jnp.logical_and(plain, jnp.logical_not(late)))
    def _():
        tell(at_h)

    @pl.when(jnp.logical_and(lower, zl >= NR + 1))
    def _():
        for t in peers:
            tell(at_x(*t, half=1))

    for copy in loads:
        copy.start()

    @pl.when(upper)
    def _():
        own.start()

    @pl.when(greets)
    def _():
        for copy in c_x:
            copy.start()

    @pl.when(quick)
    def _():
        pl.semaphore_wait(go, 1)
        for copy in f_raw:
            copy.start()

    f_whole = [make(whole.at[me], whole.at[me], send_w, recv_w, 0, int(t == (0, 1)), at_near(*t)) for t in near]
    f_z = [make(whole.at[me], whole.at[me], send_z, recv_z, int(z > 0), 0, at_z(z)) for z in range(NZ - NR)]

    f_sum = [make(part, sums.at[pair], send_s, recv_s, 0, 0, at_pair(k)) for k in range(1, NZ // 2)]
    f_direct = [make(whole.at[me], whole.at[me], send_d, recv_d, 0, 0, (0, 0))]

    def own_half():
        loads[0].wait()
        blocks(NX - 1, 1).wait_recv()
        c_c.start()

    def arrived(z):
        there = raw.at[pl.ds(z * NY, NY)]
        make(there, there, send_r, recv_r, 0, z, at_y(1)).wait_recv()

    def sums_of(n, sends, recvs, i):
        return make(whole.at[pl.ds(0, n)], whole.at[pl.ds(0, n)], sends, recvs, i, 0, at_y(1))

    @pl.when(reducer)
    def _():
        own.start()
        arrived(first_plain)
        for copy in f_raw:
            copy.start()
        own_half()

        def plane(i, total):
            z = jnp.where(i < 4, i + 3, jnp.where(i < 7, i - 4, 7))

            @pl.when(z != first_plain)
            def _():
                arrived(z)

            for j in range(NY):
                total += raw[z * NY + j].astype(F32)
            return total

        whole[me] = lax.fori_loop(0, NZ, plane, jnp.zeros((16, 128), F32))
        for copy in f_whole[:7]:
            copy.start()

        @pl.when(low == 0)
        def _():
            f_z[0].start()

        @pl.when(ten == 0)
        def _():
            for copy in f_direct:
                copy.start()

        for copy in f_z[1:] + f_whole[7:]:
            copy.start()

    @pl.when(upper)
    def _():
        total = jnp.zeros((16, 128), F32)
        for e in range(NR):
            arrived(low + e)
            for j in range(NY):
                total += raw[(low + e) * NY + j].astype(F32)
        part[...] = total
        for copy in f_sum:
            copy.start()
        sums[pair] = total

    @pl.when(jnp.logical_and(lower, jnp.logical_not(late)))
    def _():
        pl.semaphore_wait(ready, 1)
        c_h.start()

    @pl.when(jnp.logical_not(greets))
    def _():
        for copy in c_x:
            copy.start()

    chunks = whole.at[pl.ds(y * NR, NR)]
    f_y = [make(chunks, chunks, send_y, recv_y, 0, 0, at_y(k)) for k in (4, 3, 5, 2, 6, 1, 7)]
    f_skip = [jnp.logical_and(jnp.logical_and(ten == 0, zl == NR), lax.rem(y + k, NY) == 0) for k in (4, 3, 5, 2, 6, 1, 7)]

    def along_y():
        make(chunks, chunks, send_z, recv_z, 0, 0, at_y(1)).wait_recv()
        for skip, copy in zip(f_skip, f_y):

            @pl.when(jnp.logical_not(skip))
            def _():
                copy.start()

    @pl.when(jnp.logical_and(column, zl >= HUB))
    def _():
        along_y()

    c_h.wait_recv()

    @pl.when(late)
    def _():
        c_h.start()

    @pl.when(jnp.logical_not(late))
    def _():
        for copy in c_hx:
            copy.start()

    @pl.when(stand)
    def _():
        c_far.wait_recv()
        for copy in c_stand:
            copy.start()

    @pl.when(jnp.logical_and(column, zl < HUB))
    def _():
        along_y()

    @pl.when(jnp.logical_not(reducer))
    def _():
        own_half()

    f_next = f_whole[near.index((0, 1))]

    @pl.when(bridge)
    def _():
        f_next.wait_recv()
        for copy in f_y:
            copy.start()

    @pl.when(upper)
    def _():
        pairs = sums.at[pl.ds(0, NZ // 2 - 1)]
        make(pairs, pairs, send_s, recv_s, 0, 0, at_y(1)).wait_recv()
        total = sums[0]
        for i in range(1, NZ // 2):
            total += sums[i]
        whole[me] = total
        for copy in f_whole:
            copy.start()

    for copy in loads[1:5]:
        copy.wait()
    c_c.wait_recv()

    @pl.when(stand)
    def _():
        blocks(len(peers) - 1, 2).wait_recv()

    @pl.when(jnp.logical_not(stand))
    def _():
        blocks(len(peers), 2).wait_recv()

    keys = jnp.concatenate([cot[(k * NH + i) * NX + j] for i in range(NH) for j in range(NX) for k in range(NC)], axis=0)
    for i in range(4):
        rows = slice(i * 128, i * 128 + 128)
        grad = lax.dot_general(h[:, rows], keys, (((0,), (0,)), ((), ())), preferred_element_type=F32)
        first = beta_one * m[rows].astype(F32) + (1.0 - beta_one) * grad
        second = beta_two * v[rows].astype(F32) + (1.0 - beta_two) * grad * grad
        scaled = second * (1.0 / corr_two)
        root = scaled * lax.rsqrt(scaled)
        step = first * (inner_rate / corr_one) / (root + adam_eps)
        nw_ref[rows] = (w[rows].astype(F32) * (1.0 - inner_rate * decay_rate) - step).astype(BF16)
        nm_ref[rows] = first.astype(BF16)
        nv_ref[rows] = second.astype(BF16)

    c_h.wait_send()
    c_c.wait_send()
    blocks(NX - 1, 1).wait_send()
    rest = raw.at[pl.ds(0, len(near))]
    make(rest, rest, send_r, recv_r, 0, 0, at_y(1)).wait_send()

    @pl.when(jnp.logical_not(late))
    def _():
        blocks(len(peers), 2).wait_send()

    @pl.when(stand)
    def _():
        blocks(len(peers), 4).wait_send()

    @pl.when(plain)
    def _():
        f_own.wait_send()

    @pl.when(inside)
    def _():
        sums_of(len(near), send_w, recv_w, 0).wait_send()

    @pl.when(reducer)
    def _():
        sums_of(NZ - NR - 1, send_z, recv_z, 1).wait_send()

        @pl.when(low == 0)
        def _():
            f_z[0].wait_send()

        @pl.when(ten == 0)
        def _():
            f_direct[0].wait_send()

    @pl.when(upper)
    def _():
        pairs = sums.at[pl.ds(0, NZ // 2 - 1)]
        make(pairs, pairs, send_s, recv_s, 0, 0, at_y(1)).wait_send()

    fewer = jnp.logical_and(column, jnp.logical_and(ten == 0, zl == NR))

    @pl.when(fewer)
    def _():
        sums_of(NR * (NY - 2), send_y, recv_y, 0).wait_send()

    @pl.when(jnp.logical_and(jnp.logical_or(column, bridge), jnp.logical_not(fewer)))
    def _():
        sums_of(NR * (NY - 1), send_y, recv_y, 0).wait_send()

    for copy in loads[5:]:
        copy.wait()

    @pl.when(inside)
    def _():
        sums_of(len(near) - 1, send_w, recv_w, 0).wait_recv()

    @pl.when(jnp.logical_and(inside, jnp.logical_not(bridge)))
    def _():
        f_next.wait_recv()

    @pl.when(column)
    def _():
        sums_of(NR * (NY - 1), send_y, recv_y, 0).wait_recv()

    @pl.when(direct)
    def _():
        sums_of(NR * NY, send_d, recv_d, 0).wait_recv()

    for i in range(NR * NY):
        r, q = (i // 4) * 16, (i % 4) * 128
        area = (slice(r, r + 16), slice(q, q + 128))
        delta = g[area] - whole[i] * (1.0 / (NY * NZ))
        fresh = outer_mu * o[area] + delta
        no_ref[area] = fresh
        ng_ref[area] = g[area] - outer_rate * (delta + outer_mu * fresh)


def store_kernel(*refs):
    sems = refs[10]
    copies = [pltpu.make_async_copy(refs[i], refs[5 + i], sems.at[i]) for i in range(5)]
    for copy in copies:
        copy.start()
    for copy in copies:
        copy.wait()


def per_device(hidden, cotangent, weight, first, second, local, glob, momentum):
    hidden, cotangent, weight, first, second, local = (a[0] for a in (hidden, cotangent, weight, first, second, local))
    args = (hidden, cotangent, weight, first, second, local, glob, momentum)
    (tok, d), (ktok, kv), (rows, _) = hidden.shape, cotangent.shape, glob.shape
    vm = pl.BlockSpec(memory_space=pltpu.VMEM)
    out = pl.pallas_call(
        kernel,
        out_shape=[
            jax.ShapeDtypeStruct((d, kv), BF16),
            jax.ShapeDtypeStruct((d, kv), BF16),
            jax.ShapeDtypeStruct((d, kv), BF16),
            jax.ShapeDtypeStruct((rows, kv), F32),
            jax.ShapeDtypeStruct((rows, kv), F32),
        ],
        in_specs=[pl.BlockSpec(memory_space=pltpu.HBM)] * 8,
        out_specs=[vm] * 5,
        scratch_shapes=[
            pltpu.VMEM((tok, d), BF16),
            pltpu.VMEM((d, kv), BF16),
            pltpu.VMEM((d, kv), BF16),
            pltpu.VMEM((d, kv), BF16),
            pltpu.VMEM((rows, kv), F32),
            pltpu.VMEM((rows, kv), F32),
            pltpu.VMEM((NC * NH * NX, ktok, kv), BF16),
            pltpu.VMEM((NY * NZ, 16, 128), BF16),
            pltpu.VMEM((16, 128), F32),
            pltpu.VMEM((NZ // 2, 16, 128), F32),
            pltpu.VMEM((NR * NY, 16, 128), F32),
            pltpu.SemaphoreType.DMA((7,)),
            pltpu.SemaphoreType.DMA((5,)),
            pltpu.SemaphoreType.DMA((5,)),
            pltpu.SemaphoreType.DMA((2,)),
            pltpu.SemaphoreType.DMA((NZ,)),
            pltpu.SemaphoreType.DMA((1,)),
            pltpu.SemaphoreType.DMA((2,)),
            pltpu.SemaphoreType.DMA((2,)),
            pltpu.SemaphoreType.DMA((1,)),
            pltpu.SemaphoreType.DMA((1,)),
            pltpu.SemaphoreType.DMA((1,)),
            pltpu.SemaphoreType.DMA((1,)),
            pltpu.SemaphoreType.DMA((1,)),
            pltpu.SemaphoreType.DMA((1,)),
            pltpu.SemaphoreType.DMA((1,)),
            pltpu.SemaphoreType.REGULAR,
            pltpu.SemaphoreType.REGULAR,
        ],
        compiler_params=pltpu.CompilerParams(
            collective_id=0, has_side_effects=True, vmem_limit_bytes=16 * 1024 * 1024
        ),
    )(*(pltpu.with_memory_space_constraint(a, pltpu.HBM) for a in args))
    out = pl.pallas_call(
        store_kernel,
        out_shape=[jax.ShapeDtypeStruct(a.shape, a.dtype) for a in out],
        in_specs=[vm] * 5,
        out_specs=[pl.BlockSpec(memory_space=pltpu.HBM)] * 5,
        scratch_shapes=[pltpu.SemaphoreType.DMA((5,))],
        compiler_params=pltpu.CompilerParams(vmem_limit_bytes=4 * 1024 * 1024),
    )(*out)
    return (out[0][None], out[1][None], out[2][None], out[3], out[4])


def solution(mesh):
    return jax.shard_map(
        per_device,
        mesh=mesh,
        in_specs=(
            P("replica", None, "tensor"),
            P("replica", "tensor", None),
            P("replica", "tensor", None),
            P("replica", "tensor", None),
            P("replica", "tensor", None),
            P("replica", "tensor", None),
            P("tensor", None),
            P("tensor", None),
        ),
        out_specs=(
            P("replica", "tensor", None),
            P("replica", "tensor", None),
            P("replica", "tensor", None),
            P("tensor", None),
            P("tensor", None),
        ),
        check_vma=False,
    )
```

```python
import jax
import jax.numpy as jnp
from jax import lax
from jax.experimental import pallas as pl
from jax.experimental.pallas import tpu as pltpu
from jax.sharding import PartitionSpec as P

ADAM_STEP = 4
beta_one = 0.9
beta_two = 0.95
adam_eps = 1e-08
inner_rate = 0.01
decay_rate = 0.1
outer_rate = 0.7
outer_mu = 0.9
corr_one = 1.0 - beta_one**ADAM_STEP
corr_two = 1.0 - beta_two**ADAM_STEP

MESH = pl.DeviceIdType.MESH
NY, NZ, NX, NH, NC = 8, 8, 4, 2, 2
NR = 2
HUB = 4
F32 = jnp.float32
BF16 = jnp.bfloat16


def kernel(
    h_hbm, k_hbm, w_hbm, m_hbm, v_hbm, l_hbm, g_hbm, o_hbm,
    nw_ref, nm_ref, nv_ref, ng_ref, no_ref,
    h, w, m, v, g, o, cot, raw, part, sums, whole, ht, wide_w, wide_m, wide_v,
    load_sem, send_c, recv_c, send_r, recv_r, send_w, recv_w, send_z, recv_z, send_y, recv_y, send_s, recv_s, send_d, recv_d, ready, go,
):
    rep, ten = lax.axis_index("replica"), lax.axis_index("tensor")
    zl, y = rep // NY, lax.rem(rep, NY)
    zh, x, c = ten // (NX * NC), lax.rem(ten // NC, NX), lax.rem(ten, NC)
    upper = zh == 1
    lower = zh == 0
    pair = zl // 2

    def low_of(yy):
        return jnp.where(jnp.logical_and(ten == 0, yy == 0), 1, 0)

    low = jnp.where(upper, pair * 2, low_of(y))
    side = zl - low
    inside = jnp.logical_and(side >= 0, side < NR)
    reducer = jnp.logical_and(lower, inside)
    plain = jnp.logical_and(lower, jnp.logical_not(inside))
    direct = jnp.logical_and(lower, side < 0)
    column = jnp.logical_and(lower, side >= NR)
    side = lax.rem(zl + jnp.where(upper, 0, low), NR)
    bridge = jnp.logical_and(reducer, zl == NR)
    me = y * NR + side
    quick = jnp.logical_and(upper, zl < HUB)
    hub = jnp.logical_and(upper, pair == HUB // 2)
    last = jnp.logical_and(upper, pair == HUB // 2 + 1)
    greets = jnp.logical_or(upper, zl < NR + 1)
    first_plain = 3
    row = rep == 0
    late = jnp.logical_and(row, ten == 0)
    stand = jnp.logical_and(row, ten == 1)
    far = jnp.logical_and(row, ten == NX * NC)

    near = sorted(((k, e) for k in range(NY) for e in range(NR) if k + e > 0), key=lambda t: -(min(t[0], NY - t[0]) + t[1]))

    def place(k, e):
        return lax.rem(y + k, NY), (1 - side if e else side)

    def at_near(k, e):
        yy, ss = place(k, e)
        return ((jnp.where(upper, low, low_of(yy)) + ss) * NY + yy, ten)

    def at_y(k):
        return (zl * NY + lax.rem(y + k, NY), ten)

    def at_x(k, other=False, half=zh):
        return (rep, half * NX * NC + lax.rem(x + k, NX) * NC + (1 - c if other else c))

    def at_pair(k):
        return ((lax.rem(pair + k, NZ // 2) * 2 + side) * NY + y, ten)

    def at_z(z):
        return (jnp.where(z < low, z, z + NR) * NY + y, ten)

    at_h = (rep, (1 - zh) * NX * NC + x * NC + c)

    barrier = pltpu.get_barrier_semaphore()

    everyone = [(k, other) for k in (2, 1, 3, 0) for other in (False, True)]
    peers = [t for t in everyone if t != (0, False)]

    def tell(device, sem=barrier):
        pl.semaphore_signal(sem, inc=1, device_id=device, device_id_type=MESH)

    @pl.when(reducer)
    def _():
        tell(at_h)

    @pl.when(stand)
    def _():
        tell((rep, NX * NC))

    @pl.when(quick)
    def _():
        for z in (HUB, HUB + 1):
            for i in range(NY):
                tell((z * NY + i, ten))
        tell(((HUB + 2 + side) * NY + y, ten))

    @pl.when(hub)
    def _():
        tell(((HUB + 2 + side) * NY + y, ten))

    @pl.when(last)
    def _():
        tell(((HUB + side) * NY + y, ten))

    @pl.when(jnp.logical_or(hub, last))
    def _():
        for t in near:
            tell(at_near(*t))

    @pl.when(greets)
    def _():
        for t in peers:
            tell(at_x(*t))

    @pl.when(reducer)
    def _():
        for z in range(NZ - NR - 1, -1, -1):
            for i in range(NY):
                there = jnp.where(z < low_of(i), z, z + NR)
                tell((there * NY + i, ten))

    def chunk(k, e):
        yy, ss = place(k, e)
        i = yy * NR + ss
        return l_hbm.at[pl.ds(pl.multiple_of((i // 4) * 16, 16), 16), pl.ds(pl.multiple_of(lax.rem(i, 4) * 128, 128), 128)]

    loads = [
        pltpu.make_async_copy(src, dst, load_sem.at[i])
        for i, (src, dst) in enumerate([(k_hbm, cot.at[(c * NH + zh) * NX + x]), (h_hbm, h), (w_hbm, w), (m_hbm, m), (v_hbm, v), (g_hbm, g), (o_hbm, o)])
    ]
    own = pltpu.make_async_copy(chunk(0, 0), raw.at[rep], recv_r.at[zl])

    waits = (
        jnp.where(plain, NR * NY, 0)
        + jnp.where(greets, len(peers), 0)
        + jnp.where(upper, jnp.where(zl < NR + 1, 1, len(everyone)), 0)
        + jnp.where(hub, len(near) + HUB * NY + 1, 0)
        + jnp.where(last, len(near) + NZ // 2 - 1, 0)
    )
    pl.semaphore_wait(barrier, waits)

    def make(src, dst, sends, recvs, i, j, device):
        return pltpu.make_async_remote_copy(
            src_ref=src, dst_ref=dst, send_sem=sends.at[i], recv_sem=recvs.at[j], device_id=device, device_id_type=MESH
        )

    def blocks(n, i):
        return make(cot.at[pl.ds(0, n)], cot.at[pl.ds(0, n)], send_c, recv_c, i, i, at_h)

    mine = cot.at[(c * NH + zh) * NX + x]
    theirs = cot.at[(c * NH + 1 - zh) * NX + x]
    c_h = make(k_hbm, mine, send_c, recv_c, 0, 0, at_h)
    c_x = [make(k_hbm, mine, send_c, recv_c, 1, 1, at_x(k)) for k in (2, 1, 3)]
    c_hx = [make(theirs, theirs, send_c, recv_c, 2, 2, at_x(*t)) for t in peers]
    half = cot.at[pl.ds((c * NH + zh) * NX, NX)]
    c_c = make(half, half, send_c, recv_c, 3, 3, at_x(0, True))
    missed = cot.at[NX]
    c_far = make(k_hbm, missed, send_c, recv_c, 0, 4, (rep, 1))
    c_stand = [
        make(missed, missed, send_c, recv_c, 4, 0 if t == (0, True) else 2, (rep, 0 if t == (0, True) else t[0] * NC + t[1])) for t in peers
    ]

    f_raw = [make(chunk(*t), raw.at[rep], send_r, recv_r, 0, zl, at_near(*t)) for t in near]
    f_own = make(chunk(0, 0), raw.at[rep], send_r, recv_r, 1, zl, at_near(0, 0))

    @pl.when(jnp.logical_and(upper, jnp.logical_not(far)))
    def _():
        c_h.start()
        tell(at_h, ready)

    @pl.when(far)
    def _():
        c_far.start()

    @pl.when(hub)
    def _():
        for z in range(0, HUB, NR):
            tell(((z + side) * NY + y, ten), go)

    @pl.when(jnp.logical_or(plain, jnp.logical_or(hub, last)))
    def _():
        for copy in f_raw:
            copy.start()

    @pl.when(plain)
    def _():
        f_own.start()

    @pl.when(jnp.logical_and(plain, jnp.logical_not(late)))
    def _():
        tell(at_h)

    @pl.when(jnp.logical_and(lower, zl >= NR + 1))
    def _():
        for t in peers:
            tell(at_x(*t, half=1))

    for copy in loads:
        copy.start()

    @pl.when(upper)
    def _():
        own.start()

    @pl.when(greets)
    def _():
        for copy in c_x:
            copy.start()

    @pl.when(quick)
    def _():
        pl.semaphore_wait(go, 1)
        for copy in f_raw:
            copy.start()

    f_whole = [make(whole.at[me], whole.at[me], send_w, recv_w, 0, int(t == (0, 1)), at_near(*t)) for t in near]
    f_z = [make(whole.at[me], whole.at[me], send_z, recv_z, int(z > 0), 0, at_z(z)) for z in range(NZ - NR)]

    f_sum = [make(part, sums.at[pair], send_s, recv_s, 0, 0, at_pair(k)) for k in range(1, NZ // 2)]
    f_direct = [make(whole.at[me], whole.at[me], send_d, recv_d, 0, 0, (0, 0))]

    def own_half():
        loads[0].wait()
        blocks(NX - 1, 1).wait_recv()
        c_c.start()

    def arrived(z):
        there = raw.at[pl.ds(z * NY, NY)]
        make(there, there, send_r, recv_r, 0, z, at_y(1)).wait_recv()

    def sums_of(n, sends, recvs, i):
        return make(whole.at[pl.ds(0, n)], whole.at[pl.ds(0, n)], sends, recvs, i, 0, at_y(1))

    @pl.when(reducer)
    def _():
        own.start()
        arrived(first_plain)
        for copy in f_raw:
            copy.start()
        own_half()

        def plane(i, total):
            z = jnp.where(i < 4, i + 3, jnp.where(i < 7, i - 4, 7))

            @pl.when(z != first_plain)
            def _():
                arrived(z)

            for j in range(NY):
                total += raw[z * NY + j].astype(F32)
            return total

        whole[me] = lax.fori_loop(0, NZ, plane, jnp.zeros((16, 128), F32))
        for copy in f_whole[:7]:
            copy.start()

        @pl.when(low == 0)
        def _():
            f_z[0].start()

        @pl.when(ten == 0)
        def _():
            for copy in f_direct:
                copy.start()

        for copy in f_z[1:] + f_whole[7:]:
            copy.start()

    @pl.when(upper)
    def _():
        total = jnp.zeros((16, 128), F32)
        for e in range(NR):
            arrived(low + e)
            for j in range(NY):
                total += raw[(low + e) * NY + j].astype(F32)
        part[...] = total
        for copy in f_sum:
            copy.start()
        sums[pair] = total

    @pl.when(jnp.logical_and(lower, jnp.logical_not(late)))
    def _():
        pl.semaphore_wait(ready, 1)
        c_h.start()

    @pl.when(jnp.logical_not(greets))
    def _():
        for copy in c_x:
            copy.start()

    chunks = whole.at[pl.ds(y * NR, NR)]
    f_y = [make(chunks, chunks, send_y, recv_y, 0, 0, at_y(k)) for k in (4, 3, 5, 2, 6, 1, 7)]
    f_skip = [jnp.logical_and(jnp.logical_and(ten == 0, zl == NR), lax.rem(y + k, NY) == 0) for k in (4, 3, 5, 2, 6, 1, 7)]

    def along_y():
        make(chunks, chunks, send_z, recv_z, 0, 0, at_y(1)).wait_recv()
        for skip, copy in zip(f_skip, f_y):

            @pl.when(jnp.logical_not(skip))
            def _():
                copy.start()

    @pl.when(jnp.logical_and(column, zl >= HUB))
    def _():
        along_y()

    c_h.wait_recv()

    @pl.when(late)
    def _():
        c_h.start()

    @pl.when(jnp.logical_not(late))
    def _():
        for copy in c_hx:
            copy.start()

    @pl.when(stand)
    def _():
        c_far.wait_recv()
        for copy in c_stand:
            copy.start()

    @pl.when(jnp.logical_and(column, zl < HUB))
    def _():
        along_y()

    @pl.when(jnp.logical_not(reducer))
    def _():
        own_half()

    f_next = f_whole[near.index((0, 1))]

    @pl.when(bridge)
    def _():
        f_next.wait_recv()
        for copy in f_y:
            copy.start()

    @pl.when(upper)
    def _():
        pairs = sums.at[pl.ds(0, NZ // 2 - 1)]
        make(pairs, pairs, send_s, recv_s, 0, 0, at_y(1)).wait_recv()
        total = sums[0]
        for i in range(1, NZ // 2):
            total += sums[i]
        whole[me] = total
        for copy in f_whole:
            copy.start()

    for copy in loads[1:5]:
        copy.wait()
    ht[...] = h[...].T

    @pl.loop(0, 16)
    def _(i):
        rows = pl.ds(pl.multiple_of(i * 32, 32), 32)
        wide_w[rows] = w[rows].astype(F32) * (1.0 - inner_rate * decay_rate)
        wide_m[rows] = beta_one * m[rows].astype(F32)
        wide_v[rows] = beta_two * v[rows].astype(F32)

    c_c.wait_recv()

    @pl.when(stand)
    def _():
        blocks(len(peers) - 1, 2).wait_recv()

    @pl.when(jnp.logical_not(stand))
    def _():
        blocks(len(peers), 2).wait_recv()

    keys = jnp.concatenate([cot[(k * NH + i) * NX + j] for i in range(NH) for j in range(NX) for k in range(NC)], axis=0)
    for i in range(4):
        rows = slice(i * 128, i * 128 + 128)
        grad = jnp.dot(ht[rows], keys, preferred_element_type=F32)
        first = wide_m[rows] + (1.0 - beta_one) * grad
        second = wide_v[rows] + (1.0 - beta_two) * grad * grad
        scaled = second * (1.0 / corr_two)
        root = scaled * lax.rsqrt(scaled)
        step = first * (inner_rate / corr_one) / (root + adam_eps)
        nw_ref[rows] = (wide_w[rows] - step).astype(BF16)
        nm_ref[rows] = first.astype(BF16)
        nv_ref[rows] = second.astype(BF16)

    c_h.wait_send()
    c_c.wait_send()
    blocks(NX - 1, 1).wait_send()
    rest = raw.at[pl.ds(0, len(near))]
    make(rest, rest, send_r, recv_r, 0, 0, at_y(1)).wait_send()

    @pl.when(jnp.logical_not(late))
    def _():
        blocks(len(peers), 2).wait_send()

    @pl.when(stand)
    def _():
        blocks(len(peers), 4).wait_send()

    @pl.when(plain)
    def _():
        f_own.wait_send()

    @pl.when(inside)
    def _():
        sums_of(len(near), send_w, recv_w, 0).wait_send()

    @pl.when(reducer)
    def _():
        sums_of(NZ - NR - 1, send_z, recv_z, 1).wait_send()

        @pl.when(low == 0)
        def _():
            f_z[0].wait_send()

        @pl.when(ten == 0)
        def _():
            f_direct[0].wait_send()

    @pl.when(upper)
    def _():
        pairs = sums.at[pl.ds(0, NZ // 2 - 1)]
        make(pairs, pairs, send_s, recv_s, 0, 0, at_y(1)).wait_send()

    fewer = jnp.logical_and(column, jnp.logical_and(ten == 0, zl == NR))

    @pl.when(fewer)
    def _():
        sums_of(NR * (NY - 2), send_y, recv_y, 0).wait_send()

    @pl.when(jnp.logical_and(jnp.logical_or(column, bridge), jnp.logical_not(fewer)))
    def _():
        sums_of(NR * (NY - 1), send_y, recv_y, 0).wait_send()

    for copy in loads[5:]:
        copy.wait()

    @pl.when(inside)
    def _():
        sums_of(len(near) - 1, send_w, recv_w, 0).wait_recv()

    @pl.when(jnp.logical_and(inside, jnp.logical_not(bridge)))
    def _():
        f_next.wait_recv()

    @pl.when(column)
    def _():
        sums_of(NR * (NY - 1), send_y, recv_y, 0).wait_recv()

    @pl.when(direct)
    def _():
        sums_of(NR * NY, send_d, recv_d, 0).wait_recv()

    for i in range(NR * NY):
        r, q = (i // 4) * 16, (i % 4) * 128
        area = (slice(r, r + 16), slice(q, q + 128))
        delta = g[area] - whole[i] * (1.0 / (NY * NZ))
        fresh = outer_mu * o[area] + delta
        no_ref[area] = fresh
        ng_ref[area] = g[area] - outer_rate * (delta + outer_mu * fresh)


def store_kernel(*refs):
    sems = refs[10]
    copies = [pltpu.make_async_copy(refs[i], refs[5 + i], sems.at[i]) for i in range(5)]
    for copy in copies:
        copy.start()
    for copy in copies:
        copy.wait()


def per_device(hidden, cotangent, weight, first, second, local, glob, momentum):
    hidden, cotangent, weight, first, second, local = (a[0] for a in (hidden, cotangent, weight, first, second, local))
    args = (hidden, cotangent, weight, first, second, local, glob, momentum)
    (tok, d), (ktok, kv), (rows, _) = hidden.shape, cotangent.shape, glob.shape
    vm = pl.BlockSpec(memory_space=pltpu.VMEM)
    out = pl.pallas_call(
        kernel,
        out_shape=[
            jax.ShapeDtypeStruct((d, kv), BF16),
            jax.ShapeDtypeStruct((d, kv), BF16),
            jax.ShapeDtypeStruct((d, kv), BF16),
            jax.ShapeDtypeStruct((rows, kv), F32),
            jax.ShapeDtypeStruct((rows, kv), F32),
        ],
        in_specs=[pl.BlockSpec(memory_space=pltpu.HBM)] * 8,
        out_specs=[vm] * 5,
        scratch_shapes=[
            pltpu.VMEM((tok, d), BF16),
            pltpu.VMEM((d, kv), BF16),
            pltpu.VMEM((d, kv), BF16),
            pltpu.VMEM((d, kv), BF16),
            pltpu.VMEM((rows, kv), F32),
            pltpu.VMEM((rows, kv), F32),
            pltpu.VMEM((NC * NH * NX, ktok, kv), BF16),
            pltpu.VMEM((NY * NZ, 16, 128), BF16),
            pltpu.VMEM((16, 128), F32),
            pltpu.VMEM((NZ // 2, 16, 128), F32),
            pltpu.VMEM((NR * NY, 16, 128), F32),
            pltpu.VMEM((d, tok), BF16),
            pltpu.VMEM((d, kv), F32),
            pltpu.VMEM((d, kv), F32),
            pltpu.VMEM((d, kv), F32),
            pltpu.SemaphoreType.DMA((7,)),
            pltpu.SemaphoreType.DMA((5,)),
            pltpu.SemaphoreType.DMA((5,)),
            pltpu.SemaphoreType.DMA((2,)),
            pltpu.SemaphoreType.DMA((NZ,)),
            pltpu.SemaphoreType.DMA((1,)),
            pltpu.SemaphoreType.DMA((2,)),
            pltpu.SemaphoreType.DMA((2,)),
            pltpu.SemaphoreType.DMA((1,)),
            pltpu.SemaphoreType.DMA((1,)),
            pltpu.SemaphoreType.DMA((1,)),
            pltpu.SemaphoreType.DMA((1,)),
            pltpu.SemaphoreType.DMA((1,)),
            pltpu.SemaphoreType.DMA((1,)),
            pltpu.SemaphoreType.DMA((1,)),
            pltpu.SemaphoreType.REGULAR,
            pltpu.SemaphoreType.REGULAR,
        ],
        compiler_params=pltpu.CompilerParams(
            collective_id=0, has_side_effects=True, vmem_limit_bytes=16 * 1024 * 1024
        ),
    )(*(pltpu.with_memory_space_constraint(a, pltpu.HBM) for a in args))
    out = pl.pallas_call(
        store_kernel,
        out_shape=[jax.ShapeDtypeStruct(a.shape, a.dtype) for a in out],
        in_specs=[vm] * 5,
        out_specs=[pl.BlockSpec(memory_space=pltpu.HBM)] * 5,
        scratch_shapes=[pltpu.SemaphoreType.DMA((5,))],
        compiler_params=pltpu.CompilerParams(vmem_limit_bytes=4 * 1024 * 1024),
    )(*out)
    return (out[0][None], out[1][None], out[2][None], out[3], out[4])


def solution(mesh):
    return jax.shard_map(
        per_device,
        mesh=mesh,
        in_specs=(
            P("replica", None, "tensor"),
            P("replica", "tensor", None),
            P("replica", "tensor", None),
            P("replica", "tensor", None),
            P("replica", "tensor", None),
            P("replica", "tensor", None),
            P("tensor", None),
            P("tensor", None),
        ),
        out_specs=(
            P("replica", "tensor", None),
            P("replica", "tensor", None),
            P("replica", "tensor", None),
            P("tensor", None),
            P("tensor", None),
        ),
        check_vma=False,
    )
```
